32 devices in a mesh: dp: 4 (over x, core), pipe: 2 (over y), ctx: 4 (over z).
Axes of the slice: x: 2, y: 2, z: 4, core: 2. Of those that a mesh axis runs over, the one named last changes fastest.
Arguments:
- arriving: bfloat16 [2, 4, 512, 4096], P('pipe', 'dp', 'ctx'), may hold values from -6 to 6
- features: bfloat16 [2, 4, 512, 4096], P('pipe', 'dp', 'ctx'), may hold values from -6 to 6
- short_taps: float32 [2, 7, 4096], P('pipe'), may hold values from -2 to 2
- filters: float32 [2, 256, 512], P('pipe', 'ctx'), may hold values from -0.25 to 0.25
Outputs:
- feature_grads: bfloat16 [2, 4, 512, 4096], P('pipe', 'dp', 'ctx')
- filter_grads: float32 [2, 256, 512], P('pipe', 'ctx')
- tap_grads: float32 [2, 7, 4096], P('pipe', None, 'ctx')
The draws below stay inside these ranges and needn't reach their ends.
All inputs are finite; a program needn't handle non-finite values.
Results may differ from the reference program's by a relative error of at most 0.0015.
Values may be sent and summed in bfloat16 or wider, within the bound.
A program may use at most 64 MiB of HBM per device.

```python
import math
import jax
import jax.numpy as jnp
from jax import lax

C = 4096
GROUP = 16
KS = 7
SEQ = 512
SECTIONS = 2
SEQS = 4
FILTERS = 256


def block_levels(own_key, shape, shards, smallest, largest):
    factor_of, own = 1.0, jax.random.fold_in(own_key, 6)
    for position, shards_of in shards:
        heights = jnp.exp(jax.random.uniform(jax.random.fold_in(own, position), (shards_of,), jnp.float32, smallest / len(shards), largest / len(shards)))
        factor_of = factor_of * jnp.repeat(heights, shape[position] // shards_of).reshape([-1 if axis == position else 1 for axis in range(len(shape))])
    return factor_of


def normal_values(rng, dims, scale, reach, pieces=(), kind=jnp.bfloat16):
    entries = scale * jax.random.normal(rng, dims, jnp.float32)
    if pieces:
        entries = entries * block_levels(rng, dims, pieces, -0.22, 0.18)
    return jnp.clip(entries, -reach, reach).astype(kind)


def setup_inputs(seed: int = 0) -> dict:
    keys = jax.random.split(jax.random.key(seed), 5)
    return {
        "arriving": normal_values(keys[0], (SECTIONS, SEQS, SEQ, C), 1.0, 6.0, ((0, 2), (1, 4), (2, 4))),
        "features": normal_values(keys[1], (SECTIONS, SEQS, SEQ, C), 1.0, 6.0, ((0, 2), (1, 4), (2, 4))),
        "short_taps": normal_values(keys[2], (SECTIONS, KS, C), KS ** -0.5, 2.0, ((0, 2),), jnp.float32),
        "filters": normal_values(keys[3], (SECTIONS, FILTERS, SEQ), SEQ ** -0.5, 0.25, ((0, 2), (1, 4)), jnp.float32),
    }


def short_forward(tap_rows, values):
    padded = jnp.pad(values, ((KS - 1, 0), (0, 0)))
    summed = jnp.zeros(values.shape, values.dtype)
    for offset in range(KS):
        summed = summed + tap_rows[offset] * padded[KS - 1 - offset:KS - 1 - offset + SEQ]
    return summed

def short_backward(tap_rows, values):
    padded = jnp.pad(values, ((0, KS - 1), (0, 0)))
    summed = jnp.zeros(values.shape, values.dtype)
    for offset in range(KS):
        summed = summed + tap_rows[offset] * padded[offset:offset + SEQ]
    return summed

def reference(arriving, features, short_taps, filters):
    grad_out = jnp.roll(arriving, -1, axis=0)
    length = 2 * SEQ
    filter_scale = 1.0 / math.sqrt(SEQS * GROUP * SEQ)
    tap_scale = 1.0 / math.sqrt(SEQS * SEQ)

    def one_section(section_inputs):
        section_grads, section_feats, tap_rows, kernels = section_inputs
        spectrum_h = jnp.fft.rfft(kernels, n=length, axis=1)
        spectrum_h = jnp.repeat(spectrum_h, GROUP, axis=0).T

        def one_sequence(seq_inputs):
            grad_rows, feat_rows = seq_inputs
            values = feat_rows.astype(filters.dtype)
            conv_in = short_forward(tap_rows, values)
            spectrum_g = jnp.fft.rfft(grad_rows.astype(filters.dtype), n=length, axis=0)
            spectrum_u = jnp.fft.rfft(conv_in, n=length, axis=0)
            conv_in_grad = jnp.fft.irfft(jnp.conj(spectrum_h) * spectrum_g, n=length, axis=0)[:SEQ]
            lagged = jnp.fft.irfft(spectrum_g * jnp.conj(spectrum_u), n=length, axis=0)[:SEQ]
            grouped = lax.optimization_barrier(jnp.sum(lagged.reshape(SEQ, FILTERS, GROUP), axis=2)).T
            feature_grad = short_backward(tap_rows, conv_in_grad).astype(jnp.bfloat16)
            padded = jnp.pad(values, ((KS - 1, 0), (0, 0)))
            tap_terms = jnp.stack([lax.optimization_barrier(jnp.sum(conv_in_grad * padded[KS - 1 - offset:KS - 1 - offset + SEQ], axis=0)) for offset in range(KS)])
            return (feature_grad, grouped, tap_terms)
        feature_grad, grouped, tap_terms = lax.map(one_sequence, (section_grads, section_feats))
        return (feature_grad, lax.optimization_barrier(jnp.sum(grouped, axis=0)) * filter_scale, lax.optimization_barrier(jnp.sum(tap_terms, axis=0)) * tap_scale)
    feature_grads, filter_grads, tap_grads = lax.map(one_section, (grad_out, features, short_taps, filters))
    return (feature_grads, filter_grads, tap_grads)
```

```python
import functools
import math

import jax
import jax.numpy as jnp
from jax import lax
from jax.experimental import pallas as pl
from jax.experimental.pallas import tpu as pltpu
from jax.sharding import PartitionSpec as P

TABLE_PRECISION = lax.Precision.HIGH
MESH = pl.DeviceIdType.MESH


def passed_along(value, axis, steps):
    count = lax.axis_size(axis)
    pairs = [(source, (source + steps) % count) for source in range(count)]
    return lax.ppermute(value, axis, pairs)


def phase_table(count_a, count_b, modulus):
    first_index = lax.broadcasted_iota(jnp.int32, (count_a, count_b), 0)
    second_index = lax.broadcasted_iota(jnp.int32, (count_a, count_b), 1)
    phase = (first_index * second_index % modulus).astype(jnp.float32) * (2.0 * math.pi / modulus)
    return (jnp.cos(phase), jnp.sin(phase))


def block_table(cos_part, sin_part):
    return jnp.stack(
        [
            jnp.concatenate([cos_part, -sin_part], axis=-1),
            jnp.concatenate([sin_part, cos_part], axis=-1),
        ]
    )


def split_length(seq_len):
    factor = 1
    for candidate in range(1, seq_len + 1):
        if seq_len % candidate == 0 and candidate * candidate <= 2 * seq_len:
            factor = candidate
    return factor


def finish_forward(first, inner_len, outer_len):
    full_len = inner_len * outer_len
    cos_turn, sin_turn = phase_table(inner_len, outer_len, full_len)
    first_re = first[..., :outer_len]
    first_im = first[..., outer_len:]
    turned = jnp.stack(
        [first_re * cos_turn + first_im * sin_turn, first_im * cos_turn - first_re * sin_turn],
        axis=-3,
    )
    cos_last, sin_last = phase_table(inner_len, inner_len, inner_len)
    return jnp.einsum(
        "...cnk,cne->...ke", turned, block_table(cos_last, sin_last), precision=TABLE_PRECISION
    )


def forward_pairs(values):
    inner_len = values.shape[-1]
    half_rows = values.shape[-2]
    outer_len = 2 * half_rows
    cos_first, sin_first = phase_table(half_rows, outer_len, outer_len)
    first = jnp.einsum(
        "fagmn,ame->fgne", values, block_table(cos_first, sin_first), precision=TABLE_PRECISION
    )
    return finish_forward(first, inner_len, outer_len)


def forward_real(values):
    inner_len = values.shape[-1]
    half_rows = values.shape[-2]
    outer_len = 2 * half_rows
    cos_first, sin_first = phase_table(half_rows, outer_len, outer_len)
    first = jnp.einsum(
        "fmn,me->fne", values, block_table(cos_first, sin_first)[0], precision=TABLE_PRECISION
    )
    return finish_forward(first, inner_len, outer_len)


def inverse_spectrum(spectrum, real_only):
    outer_len = spectrum.shape[-2]
    inner_len = spectrum.shape[-1] // 2
    half_rows = outer_len // 2
    full_len = outer_len * inner_len
    cos_first, sin_first = phase_table(inner_len, inner_len, inner_len)
    table_first = jnp.concatenate(
        [
            jnp.concatenate([cos_first, sin_first], axis=1),
            jnp.concatenate([-sin_first, cos_first], axis=1),
        ],
        axis=0,
    )
    step = jnp.einsum("...ke,ew->...kw", spectrum, table_first, precision=TABLE_PRECISION)
    step_re = step[..., :inner_len]
    step_im = step[..., inner_len:]
    cos_turn, sin_turn = phase_table(outer_len, inner_len, full_len)
    turned = jnp.stack(
        [step_re * cos_turn - step_im * sin_turn, step_re * sin_turn + step_im * cos_turn], axis=-3
    )
    cos_last, sin_last = phase_table(half_rows, outer_len, outer_len)
    table_last = jnp.stack(
        [jnp.stack([cos_last, -sin_last], axis=1), jnp.stack([sin_last, cos_last], axis=1)]
    )
    norm_factor = 1.0 / full_len
    if real_only:
        return (
            jnp.einsum("mck,...ckn->m...n", table_last[0], turned, precision=TABLE_PRECISION)
            * norm_factor
        )
    return (
        jnp.einsum("dmck,...ckn->dm...n", table_last, turned, precision=TABLE_PRECISION)
        * norm_factor
    )


def body(arriving, features, short_taps, filters):
    ctx_count = lax.axis_size("ctx")
    ctx_rank = lax.axis_index("ctx")
    dp_count = lax.axis_size("dp")
    rows_dev = features.shape[2]
    channels = features.shape[3]
    own_width = channels // ctx_count
    filter_count = filters.shape[1]
    group_size = own_width // filter_count
    half_group = group_size // 2
    taps_count = short_taps.shape[1]
    seq_len = filters.shape[2]
    inner_len = split_length(seq_len)
    half_rows = seq_len // inner_len
    feature_cols = features[0, 0].T
    arrived = passed_along(arriving, "pipe", -1)
    gradient_cols = arrived[0, 0].T
    gradient_block, feature_block = (
        lax.all_to_all(gradient_cols, "ctx", split_axis=0, concat_axis=1, tiled=True),
        lax.all_to_all(feature_cols, "ctx", split_axis=0, concat_axis=1, tiled=True),
    )
    tap_block = lax.dynamic_slice_in_dim(short_taps[0], ctx_rank * own_width, own_width, 1)
    feature_vals = feature_block.astype(jnp.float32)
    padded_feat = jnp.pad(feature_vals, ((0, 0), (taps_count - 1, 0)))
    conv_in = jnp.zeros(feature_vals.shape, jnp.float32)
    for offset in range(taps_count):
        conv_in = (
            conv_in
            + tap_block[offset][:, None]
            * padded_feat[:, taps_count - 1 - offset : taps_count - 1 - offset + seq_len]
        )
    pair_shape = (filter_count, 2, half_group, half_rows, inner_len)
    spectrum_u = forward_pairs(conv_in.reshape(pair_shape))
    spectrum_g = forward_pairs(gradient_block.astype(jnp.float32).reshape(pair_shape))
    spectrum_h = forward_real(filters[0].reshape(filter_count, half_rows, inner_len))[:, None]
    g_re = spectrum_g[..., :inner_len]
    g_im = spectrum_g[..., inner_len:]
    u_re = spectrum_u[..., :inner_len]
    u_im = spectrum_u[..., inner_len:]
    h_re = spectrum_h[..., :inner_len]
    h_im = spectrum_h[..., inner_len:]
    back = jnp.concatenate([h_re * g_re + h_im * g_im, h_re * g_im - h_im * g_re], axis=-1)
    lag = jnp.concatenate(
        [jnp.sum(g_re * u_re + g_im * u_im, axis=1), jnp.sum(g_im * u_re - g_re * u_im, axis=1)],
        axis=-1,
    )
    grad_blocks = inverse_spectrum(back, False)
    conv_in_grad = jnp.transpose(grad_blocks, (2, 0, 3, 1, 4)).reshape(own_width, seq_len)
    filter_part = jnp.transpose(inverse_spectrum(lag, True), (1, 0, 2)).reshape(
        filter_count, seq_len
    )
    padded_grad = jnp.pad(conv_in_grad, ((0, 0), (0, taps_count - 1)))
    feature_grad = jnp.zeros(conv_in_grad.shape, jnp.float32)
    tap_terms = []
    for offset in range(taps_count):
        feature_grad = (
            feature_grad + tap_block[offset][:, None] * padded_grad[:, offset : offset + seq_len]
        )
        tap_terms.append(
            jnp.sum(
                conv_in_grad
                * padded_feat[:, taps_count - 1 - offset : taps_count - 1 - offset + seq_len],
                axis=1,
            )
        )
    tap_part = jnp.stack(tap_terms)
    filter_total, tap_total = lax.psum((filter_part, tap_part), "dp")
    back_cols = feature_grad.astype(jnp.bfloat16)
    feature_rows = lax.all_to_all(back_cols, "ctx", split_axis=1, concat_axis=0, tiled=True)
    feature_grads = feature_rows.T.reshape(1, 1, rows_dev, channels)
    filter_scale = 1.0 / math.sqrt(dp_count * group_size * seq_len)
    tap_scale = 1.0 / math.sqrt(dp_count * seq_len)
    filter_grads = (filter_total * filter_scale)[None]
    tap_grads = (tap_total * tap_scale).reshape(1, taps_count, own_width)
    return (feature_grads, filter_grads, tap_grads)


def fused_kernel(
    sizes,
    arriving,
    features,
    taps,
    filters,
    feature_out,
    filter_out,
    tap_out,
    inbox,
    outbox,
    shares,
    wide_feat,
    split_in,
    pair_grad,
    twin_grad,
    conv_grad,
    diagonals,
    send_in,
    recv_in,
    send_out,
    recv_out,
    send_share,
    recv_share,
):
    blocks, dp_count, pipe_count, chunks, rows, width, group, taps_count = sizes
    seq_len = blocks * rows
    own_width = chunks * width
    per_chunk = width // group
    me = lax.axis_index("ctx")
    dp_rank = lax.axis_index("dp")
    pipe_rank = lax.axis_index("pipe")
    before = lax.rem(pipe_rank + pipe_count - 1, pipe_count)

    barrier = pltpu.get_barrier_semaphore()
    for step in range(1, blocks):
        pl.semaphore_signal(
            barrier,
            inc=1,
            device_id={"ctx": lax.rem(me + step, blocks)},
            device_id_type=MESH,
        )
    for step in range(blocks):
        pl.semaphore_signal(
            barrier,
            inc=1,
            device_id={"pipe": before, "ctx": lax.rem(me + step, blocks)},
            device_id_type=MESH,
        )
    for step in range(1, dp_count):
        pl.semaphore_signal(
            barrier,
            inc=1,
            device_id={"dp": lax.rem(dp_rank + step, dp_count)},
            device_id_type=MESH,
        )
    pl.semaphore_wait(barrier, 2 * blocks + dp_count - 2)

    def columns(owner, chunk):
        return pl.ds(pl.multiple_of(owner * own_width + chunk * width, width), width)

    def send_chunk(chunk, carry):
        for step in range(blocks):
            target = lax.rem(me + step, blocks)
            pltpu.make_async_remote_copy(
                src_ref=arriving.at[:, columns(target, chunk)],
                dst_ref=inbox.at[chunk, blocks + me],
                send_sem=send_in,
                recv_sem=recv_in.at[chunk],
                device_id={"pipe": before, "ctx": target},
                device_id_type=MESH,
            ).start()
            if step:
                pltpu.make_async_remote_copy(
                    src_ref=features.at[:, columns(target, chunk)],
                    dst_ref=inbox.at[chunk, me],
                    send_sem=send_in,
                    recv_sem=recv_in.at[chunk],
                    device_id={"ctx": target},
                    device_id_type=MESH,
                ).start()
        pltpu.make_async_copy(
            features.at[:, columns(me, chunk)], inbox.at[chunk, me], recv_in.at[chunk]
        ).start()
        return carry

    lax.fori_loop(0, chunks, send_chunk, 0)

    wide_feat[0:8, :] = jnp.zeros((8, width), jnp.float32)
    conv_grad[seq_len : seq_len + 8, :] = jnp.zeros((8, width), jnp.float32)
    row_index = lax.broadcasted_iota(jnp.int32, (rows, rows), 0)
    lane_index = lax.broadcasted_iota(jnp.int32, (rows, rows), 1)
    upper = lane_index >= row_index
    lane_group = lane_index // group
    zero_tile = jnp.zeros((rows, rows), jnp.float32)

    def do_chunk(chunk, carry):
        pltpu.make_async_copy(inbox.at[chunk], inbox.at[chunk], recv_in.at[chunk]).wait()
        tap_rows = taps[:, columns(me, chunk)]
        for block in range(blocks):
            wide_feat[8 + block * rows : 8 + (block + 1) * rows, :] = inbox[chunk, block].astype(
                jnp.float32
            )
        for block in range(blocks):
            here = slice(block * rows, (block + 1) * rows)
            summed = zero_tile
            for tap in range(taps_count):
                start = 8 + block * rows - tap
                summed = summed + tap_rows[tap : tap + 1] * wide_feat[start : start + rows, :]
            high = summed.astype(jnp.bfloat16)
            low = (summed - high.astype(jnp.float32)).astype(jnp.bfloat16)
            split_in[here, 0:width] = high
            split_in[here, width : 2 * width] = low
            grad = inbox[chunk, blocks + block]
            twin_grad[here, 0:width] = grad
            twin_grad[here, width : 2 * width] = grad
            pair_grad[here, 0:width] = grad
            if block:
                pair_grad[(block - 1) * rows : block * rows, width : 2 * width] = grad
        pair_grad[seq_len - rows : seq_len, width : 2 * width] = jnp.zeros(
            (rows, width), jnp.bfloat16
        )

        def do_filter(index, inner):
            ours = lane_group == index
            kernel_row = filters[pl.ds(chunk * per_chunk + index, 1), :]
            highs, lows = [], []
            last = zero_tile
            for block in range(blocks):
                spread = jnp.broadcast_to(
                    kernel_row[:, block * rows : (block + 1) * rows], (rows, rows)
                )
                rolled = pltpu.roll(spread, 0, 1, stride=1, stride_axis=0)
                tile = jnp.where(upper, rolled, last)
                last = rolled
                high = tile.astype(jnp.bfloat16)
                highs.append(high)
                lows.append((tile - high.astype(jnp.float32)).astype(jnp.bfloat16))
            table = jnp.concatenate(
                [jnp.concatenate(highs, axis=1), jnp.concatenate(lows, axis=1)], axis=0
            )
            for block in range(0, blocks, 2):
                product = jnp.dot(
                    table[:, : seq_len - block * rows],
                    pair_grad[block * rows :, :],
                    preferred_element_type=jnp.float32,
                )
                both = product[:rows] + product[rows:]
                for half in range(2):
                    here = slice((block + half) * rows, (block + half + 1) * rows)
                    conv_grad[here, :] = jnp.where(
                        ours, both[:, half * width : (half + 1) * width], conv_grad[here, :]
                    )
            ours_twice = jnp.concatenate([ours, ours], axis=1)
            picked = [
                jnp.where(
                    ours_twice,
                    split_in[block * rows : (block + 1) * rows, :],
                    jnp.zeros((rows, 2 * width), jnp.bfloat16),
                )
                for block in range(blocks)
            ]
            sums = [None] * blocks
            for block in range(0, blocks, 2):
                product = lax.dot_general(
                    jnp.concatenate(picked[: block + 2], axis=0),
                    twin_grad[block * rows : (block + 2) * rows, :],
                    (((1,), (1,)), ((), ())),
                    preferred_element_type=jnp.float32,
                )
                for half in range(2):
                    for early in range(block + half + 1):
                        lag = block + half - early
                        piece = product[
                            early * rows : (early + 1) * rows, half * rows : (half + 1) * rows
                        ]
                        sums[lag] = piece if sums[lag] is None else sums[lag] + piece
            for lag in range(blocks):
                following = sums[lag + 1] if lag + 1 < blocks else zero_tile
                merged = jnp.where(upper, sums[lag], following)
                folded = merged[0:8]
                for part in range(1, rows // 8):
                    folded = folded + pltpu.roll(
                        merged[part * 8 : part * 8 + 8], rows - part * 8, 1
                    )
                place = pl.multiple_of((lag * per_chunk + index) * 8, 8)
                diagonals[pl.ds(place, 8), :] = folded
            return inner

        lax.fori_loop(0, per_chunk, do_filter, 0)

        lagged = diagonals[pl.ds(0, blocks * per_chunk, stride=8), :]
        for turn in range(1, 8):
            lagged = lagged + pltpu.roll(
                diagonals[pl.ds(turn, blocks * per_chunk, stride=8), :], rows - turn, 1
            )
        for lag in range(blocks):
            shares[dp_rank, chunk, :, lag * rows : (lag + 1) * rows] = lagged[
                lag * per_chunk : (lag + 1) * per_chunk
            ]
        tap_sums = [jnp.zeros((1, width), jnp.float32)] * taps_count
        for block in range(blocks):
            here = block * rows
            summed = zero_tile
            grads = conv_grad[here : here + rows, :]
            for tap in range(taps_count):
                summed = summed + tap_rows[tap : tap + 1] * conv_grad[here + tap : here + tap + rows, :]
                start = 8 + here - tap
                tap_sums[tap] = tap_sums[tap] + jnp.sum(
                    grads * wide_feat[start : start + rows, :], axis=0, keepdims=True
                )
            outbox[chunk, block] = summed.astype(jnp.bfloat16)
        filler = [jnp.zeros((per_chunk - taps_count, width), jnp.float32)]
        shares[dp_rank, chunk, :, seq_len : seq_len + width] = jnp.concatenate(
            tap_sums + (filler if per_chunk > taps_count else []), axis=0
        )
        for step in range(1, blocks):
            target = lax.rem(me + step, blocks)
            pltpu.make_async_remote_copy(
                src_ref=outbox.at[chunk, target],
                dst_ref=feature_out.at[:, columns(me, chunk)],
                send_sem=send_out,
                recv_sem=recv_out,
                device_id={"ctx": target},
                device_id_type=MESH,
            ).start()
        pltpu.make_async_copy(
            outbox.at[chunk, me], feature_out.at[:, columns(me, chunk)], recv_out
        ).start()
        for step in range(1, dp_count):
            pltpu.make_async_remote_copy(
                src_ref=shares.at[dp_rank, chunk],
                dst_ref=shares.at[dp_rank, chunk],
                send_sem=send_share,
                recv_sem=recv_share,
                device_id={"dp": lax.rem(dp_rank + step, dp_count)},
                device_id_type=MESH,
            ).start()
        return carry

    lax.fori_loop(0, chunks, do_chunk, 0)

    others = shares.at[0 : dp_count - 1]
    pltpu.make_async_copy(others, others, recv_share).wait()
    pltpu.make_async_copy(others, others, send_share).wait()
    filter_scale = 1.0 / math.sqrt(dp_count * group * seq_len)
    tap_scale = 1.0 / math.sqrt(dp_count * seq_len)
    for chunk in range(chunks):
        total = shares[0, chunk]
        for rank in range(1, dp_count):
            total = total + shares[rank, chunk]
        filter_out[chunk * per_chunk : (chunk + 1) * per_chunk, :] = (
            total[:, :seq_len] * filter_scale
        )
        tap_out[:, chunk * width : (chunk + 1) * width] = (
            total[:taps_count, seq_len:] * tap_scale
        )
    inputs_sent = inbox.at[:, 0 : 2 * blocks - 1]
    pltpu.make_async_copy(inputs_sent, inputs_sent, send_in).wait()
    outputs_sent = outbox.at[:, 0 : blocks - 1]
    pltpu.make_async_copy(outputs_sent, outputs_sent, send_out).wait()
    pltpu.make_async_copy(outbox, outbox, recv_out).wait()


def fused_body(arriving, features, short_taps, filters):
    blocks = lax.axis_size("ctx")
    dp_count = lax.axis_size("dp")
    pipe_count = lax.axis_size("pipe")
    rows, channels = features.shape[2], features.shape[3]
    own_width = channels // blocks
    filter_count, seq_len = filters.shape[1], filters.shape[2]
    group = own_width // filter_count
    taps_count = short_taps.shape[1]
    width = rows
    chunks = own_width // width
    per_chunk = width // group
    sizes = (blocks, dp_count, pipe_count, chunks, rows, width, group, taps_count)
    anywhere = pl.BlockSpec(memory_space=pl.ANY)
    vmem = pl.BlockSpec(memory_space=pltpu.VMEM)
    feature_grads, filter_grads, tap_grads = pl.pallas_call(
        functools.partial(fused_kernel, sizes),
        out_shape=(
            jax.ShapeDtypeStruct((rows, channels), jnp.bfloat16),
            jax.ShapeDtypeStruct((filter_count, seq_len), jnp.float32),
            jax.ShapeDtypeStruct((taps_count, own_width), jnp.float32),
        ),
        in_specs=[anywhere, anywhere, vmem, vmem],
        out_specs=(anywhere, vmem, vmem),
        scratch_shapes=[
            pltpu.VMEM((chunks, 2 * blocks, rows, width), jnp.bfloat16),
            pltpu.VMEM((chunks, blocks, rows, width), jnp.bfloat16),
            pltpu.VMEM((dp_count, chunks, per_chunk, seq_len + width), jnp.float32),
            pltpu.VMEM((seq_len + 8, width), jnp.float32),
            pltpu.VMEM((seq_len, 2 * width), jnp.bfloat16),
            pltpu.VMEM((seq_len, 2 * width), jnp.bfloat16),
            pltpu.VMEM((seq_len, 2 * width), jnp.bfloat16),
            pltpu.VMEM((seq_len + 8, width), jnp.float32),
            pltpu.VMEM((blocks * per_chunk * 8, width), jnp.float32),
            pltpu.SemaphoreType.DMA,
            pltpu.SemaphoreType.DMA((chunks,)),
            pltpu.SemaphoreType.DMA,
            pltpu.SemaphoreType.DMA,
            pltpu.SemaphoreType.DMA,
            pltpu.SemaphoreType.DMA,
        ],
        compiler_params=pltpu.CompilerParams(
            collective_id=0, has_side_effects=True, vmem_limit_bytes=32 * 1024 * 1024
        ),
    )(arriving[0, 0], features[0, 0], short_taps[0], filters[0])
    return (feature_grads[None, None], filter_grads[None], tap_grads[None])


def fits_fused(mesh, features, short_taps, filters):
    blocks, rows = mesh.shape["ctx"], features.shape[2] // mesh.shape["ctx"]
    own_width = features.shape[3] // blocks
    own_filters = filters.shape[1] // blocks
    group = own_width // own_filters
    return (
        rows == 128
        and blocks % 2 == 0
        and blocks <= 8
        and mesh.shape["pipe"] == 2
        and own_width % rows == 0
        and rows % group == 0
        and rows // group == 8
        and short_taps.shape[1] <= 8
    )


def solution(mesh):
    in_specs = (
        P("pipe", "dp", "ctx", None),
        P("pipe", "dp", "ctx", None),
        P("pipe", None, None),
        P("pipe", "ctx", None),
    )
    out_specs = (P("pipe", "dp", "ctx", None), P("pipe", "ctx", None), P("pipe", None, "ctx"))

    def run(arriving, features, short_taps, filters):
        chosen = fused_body if fits_fused(mesh, features, short_taps, filters) else body
        return jax.shard_map(
            chosen, mesh=mesh, in_specs=in_specs, out_specs=out_specs, check_vma=False
        )(arriving, features, short_taps, filters)

    return run
```

```python
import functools
import math

import jax
import jax.numpy as jnp
from jax import lax
from jax.experimental import pallas as pl
from jax.experimental.pallas import tpu as pltpu
from jax.sharding import PartitionSpec as P

TABLE_PRECISION = lax.Precision.HIGH
MESH = pl.DeviceIdType.MESH


def passed_along(value, axis, steps):
    count = lax.axis_size(axis)
    pairs = [(source, (source + steps) % count) for source in range(count)]
    return lax.ppermute(value, axis, pairs)


def phase_table(count_a, count_b, modulus):
    first_index = lax.broadcasted_iota(jnp.int32, (count_a, count_b), 0)
    second_index = lax.broadcasted_iota(jnp.int32, (count_a, count_b), 1)
    phase = (first_index * second_index % modulus).astype(jnp.float32) * (2.0 * math.pi / modulus)
    return (jnp.cos(phase), jnp.sin(phase))


def block_table(cos_part, sin_part):
    return jnp.stack(
        [
            jnp.concatenate([cos_part, -sin_part], axis=-1),
            jnp.concatenate([sin_part, cos_part], axis=-1),
        ]
    )


def split_length(seq_len):
    factor = 1
    for candidate in range(1, seq_len + 1):
        if seq_len % candidate == 0 and candidate * candidate <= 2 * seq_len:
            factor = candidate
    return factor


def finish_forward(first, inner_len, outer_len):
    full_len = inner_len * outer_len
    cos_turn, sin_turn = phase_table(inner_len, outer_len, full_len)
    first_re = first[..., :outer_len]
    first_im = first[..., outer_len:]
    turned = jnp.stack(
        [first_re * cos_turn + first_im * sin_turn, first_im * cos_turn - first_re * sin_turn],
        axis=-3,
    )
    cos_last, sin_last = phase_table(inner_len, inner_len, inner_len)
    return jnp.einsum(
        "...cnk,cne->...ke", turned, block_table(cos_last, sin_last), precision=TABLE_PRECISION
    )


def forward_pairs(values):
    inner_len = values.shape[-1]
    half_rows = values.shape[-2]
    outer_len = 2 * half_rows
    cos_first, sin_first = phase_table(half_rows, outer_len, outer_len)
    first = jnp.einsum(
        "fagmn,ame->fgne", values, block_table(cos_first, sin_first), precision=TABLE_PRECISION
    )
    return finish_forward(first, inner_len, outer_len)


def forward_real(values):
    inner_len = values.shape[-1]
    half_rows = values.shape[-2]
    outer_len = 2 * half_rows
    cos_first, sin_first = phase_table(half_rows, outer_len, outer_len)
    first = jnp.einsum(
        "fmn,me->fne", values, block_table(cos_first, sin_first)[0], precision=TABLE_PRECISION
    )
    return finish_forward(first, inner_len, outer_len)


def inverse_spectrum(spectrum, real_only):
    outer_len = spectrum.shape[-2]
    inner_len = spectrum.shape[-1] // 2
    half_rows = outer_len // 2
    full_len = outer_len * inner_len
    cos_first, sin_first = phase_table(inner_len, inner_len, inner_len)
    table_first = jnp.concatenate(
        [
            jnp.concatenate([cos_first, sin_first], axis=1),
            jnp.concatenate([-sin_first, cos_first], axis=1),
        ],
        axis=0,
    )
    step = jnp.einsum("...ke,ew->...kw", spectrum, table_first, precision=TABLE_PRECISION)
    step_re = step[..., :inner_len]
    step_im = step[..., inner_len:]
    cos_turn, sin_turn = phase_table(outer_len, inner_len, full_len)
    turned = jnp.stack(
        [step_re * cos_turn - step_im * sin_turn, step_re * sin_turn + step_im * cos_turn], axis=-3
    )
    cos_last, sin_last = phase_table(half_rows, outer_len, outer_len)
    table_last = jnp.stack(
        [jnp.stack([cos_last, -sin_last], axis=1), jnp.stack([sin_last, cos_last], axis=1)]
    )
    norm_factor = 1.0 / full_len
    if real_only:
        return (
            jnp.einsum("mck,...ckn->m...n", table_last[0], turned, precision=TABLE_PRECISION)
            * norm_factor
        )
    return (
        jnp.einsum("dmck,...ckn->dm...n", table_last, turned, precision=TABLE_PRECISION)
        * norm_factor
    )


def body(arriving, features, short_taps, filters):
    ctx_count = lax.axis_size("ctx")
    ctx_rank = lax.axis_index("ctx")
    dp_count = lax.axis_size("dp")
    rows_dev = features.shape[2]
    channels = features.shape[3]
    own_width = channels // ctx_count
    filter_count = filters.shape[1]
    group_size = own_width // filter_count
    half_group = group_size // 2
    taps_count = short_taps.shape[1]
    seq_len = filters.shape[2]
    inner_len = split_length(seq_len)
    half_rows = seq_len // inner_len
    feature_cols = features[0, 0].T
    arrived = passed_along(arriving, "pipe", -1)
    gradient_cols = arrived[0, 0].T
    gradient_block, feature_block = (
        lax.all_to_all(gradient_cols, "ctx", split_axis=0, concat_axis=1, tiled=True),
        lax.all_to_all(feature_cols, "ctx", split_axis=0, concat_axis=1, tiled=True),
    )
    tap_block = lax.dynamic_slice_in_dim(short_taps[0], ctx_rank * own_width, own_width, 1)
    feature_vals = feature_block.astype(jnp.float32)
    padded_feat = jnp.pad(feature_vals, ((0, 0), (taps_count - 1, 0)))
    conv_in = jnp.zeros(feature_vals.shape, jnp.float32)
    for offset in range(taps_count):
        conv_in = (
            conv_in
            + tap_block[offset][:, None]
            * padded_feat[:, taps_count - 1 - offset : taps_count - 1 - offset + seq_len]
        )
    pair_shape = (filter_count, 2, half_group, half_rows, inner_len)
    spectrum_u = forward_pairs(conv_in.reshape(pair_shape))
    spectrum_g = forward_pairs(gradient_block.astype(jnp.float32).reshape(pair_shape))
    spectrum_h = forward_real(filters[0].reshape(filter_count, half_rows, inner_len))[:, None]
    g_re = spectrum_g[..., :inner_len]
    g_im = spectrum_g[..., inner_len:]
    u_re = spectrum_u[..., :inner_len]
    u_im = spectrum_u[..., inner_len:]
    h_re = spectrum_h[..., :inner_len]
    h_im = spectrum_h[..., inner_len:]
    back = jnp.concatenate([h_re * g_re + h_im * g_im, h_re * g_im - h_im * g_re], axis=-1)
    lag = jnp.concatenate(
        [jnp.sum(g_re * u_re + g_im * u_im, axis=1), jnp.sum(g_im * u_re - g_re * u_im, axis=1)],
        axis=-1,
    )
    grad_blocks = inverse_spectrum(back, False)
    conv_in_grad = jnp.transpose(grad_blocks, (2, 0, 3, 1, 4)).reshape(own_width, seq_len)
    filter_part = jnp.transpose(inverse_spectrum(lag, True), (1, 0, 2)).reshape(
        filter_count, seq_len
    )
    padded_grad = jnp.pad(conv_in_grad, ((0, 0), (0, taps_count - 1)))
    feature_grad = jnp.zeros(conv_in_grad.shape, jnp.float32)
    tap_terms = []
    for offset in range(taps_count):
        feature_grad = (
            feature_grad + tap_block[offset][:, None] * padded_grad[:, offset : offset + seq_len]
        )
        tap_terms.append(
            jnp.sum(
                conv_in_grad
                * padded_feat[:, taps_count - 1 - offset : taps_count - 1 - offset + seq_len],
                axis=1,
            )
        )
    tap_part = jnp.stack(tap_terms)
    filter_total, tap_total = lax.psum((filter_part, tap_part), "dp")
    back_cols = feature_grad.astype(jnp.bfloat16)
    feature_rows = lax.all_to_all(back_cols, "ctx", split_axis=1, concat_axis=0, tiled=True)
    feature_grads = feature_rows.T.reshape(1, 1, rows_dev, channels)
    filter_scale = 1.0 / math.sqrt(dp_count * group_size * seq_len)
    tap_scale = 1.0 / math.sqrt(dp_count * seq_len)
    filter_grads = (filter_total * filter_scale)[None]
    tap_grads = (tap_total * tap_scale).reshape(1, taps_count, own_width)
    return (feature_grads, filter_grads, tap_grads)


def fused_kernel(
    sizes,
    arriving,
    features,
    taps_all,
    filters_all,
    feature_out,
    filter_out,
    tap_out,
    taps,
    filters,
    lent_filters,
    inbox,
    late_inbox,
    late_edge,
    outbox,
    late_outbox,
    shares,
    late_share,
    late_landed,
    wide_feat,
    split_in,
    pair_grad,
    twin_grad,
    conv_grad,
    diagonals,
    local_sems,
    send_in,
    recv_in,
    recv_late,
    send_edge,
    recv_edge,
    send_lent,
    recv_lent,
    send_late,
    recv_landed,
    send_out,
    recv_out,
    send_share,
    recv_share,
):
    blocks, dp_count, pipe_count, chunks, rows, width, group, taps_count = sizes
    seq_len = blocks * rows
    half = blocks // 2
    own_width = chunks * width
    per_chunk = width // group
    me = lax.axis_index("ctx")
    dp_rank = lax.axis_index("dp")
    pipe_rank = lax.axis_index("pipe")
    before = lax.rem(pipe_rank + pipe_count - 1, pipe_count)
    is_early = me < half
    is_late = me >= half

    fetch_taps = pltpu.make_async_copy(taps_all, taps, local_sems.at[0])
    fetch_taps.start()
    fetch_filters = pltpu.make_async_copy(filters_all.at[0], filters, local_sems.at[1])
    fetch_filters.start()

    barrier = pltpu.get_barrier_semaphore()
    for step in range(1, blocks):
        pl.semaphore_signal(
            barrier,
            inc=1,
            device_id={"ctx": lax.rem(me + step, blocks)},
            device_id_type=MESH,
        )
    for step in range(blocks):
        pl.semaphore_signal(
            barrier,
            inc=1,
            device_id={"pipe": before, "ctx": lax.rem(me + step, blocks)},
            device_id_type=MESH,
        )
    for step in range(1, dp_count):
        pl.semaphore_signal(
            barrier,
            inc=1,
            device_id={"dp": lax.rem(dp_rank + step, dp_count)},
            device_id_type=MESH,
        )
    pl.semaphore_wait(barrier, 2 * blocks + dp_count - 2)

    def columns(owner, chunk):
        return pl.ds(pl.multiple_of(owner * own_width + chunk * width, width), width)

    def tap_rows_of(owner, chunk):
        place = owner * chunks + chunk
        return [taps[tap, pl.ds(place, 1), :] for tap in range(taps_count)]

    def send(source, target, send_sem, recv_sem, device):
        pltpu.make_async_remote_copy(
            src_ref=source,
            dst_ref=target,
            send_sem=send_sem,
            recv_sem=recv_sem,
            device_id=device,
            device_id_type=MESH,
        ).start()

    def send_chunk(chunk, carry):
        @pl.when(is_early)
        def _():
            send(
                filters_all.at[0, pl.ds(pl.multiple_of(chunk * per_chunk, 8), per_chunk), 0 : half * rows],
                lent_filters.at[chunk],
                send_lent,
                recv_lent.at[chunk],
                {"ctx": me + half},
            )

        @pl.when(me == half - 1)
        def _():
            for owner in range(half):
                send(
                    features.at[rows - 16 : rows, columns(owner, chunk)],
                    late_edge.at[chunk],
                    send_edge,
                    recv_edge.at[chunk],
                    {"ctx": half + owner},
                )

        @pl.when(is_late)
        def _():
            for step in range(half):
                owner = lax.rem(me + step, half)
                device = owner + half
                send(
                    arriving.at[:, columns(owner, chunk)],
                    late_inbox.at[chunk, me - half],
                    send_in,
                    recv_late.at[chunk],
                    {"pipe": before, "ctx": device},
                )
                if step:
                    send(
                        features.at[:, columns(owner, chunk)],
                        late_inbox.at[chunk, me],
                        send_in,
                        recv_late.at[chunk],
                        {"ctx": device},
                    )
                else:
                    pltpu.make_async_copy(
                        features.at[:, columns(owner, chunk)],
                        late_inbox.at[chunk, me],
                        recv_late.at[chunk],
                    ).start()

        for step in range(blocks):
            target = lax.rem(me + step, blocks)
            send(
                arriving.at[:, columns(target, chunk)],
                inbox.at[chunk, me],
                send_in,
                recv_in.at[chunk],
                {"pipe": before, "ctx": target},
            )
            if step:

                @pl.when(jnp.logical_or(is_early, target >= half))
                def _():
                    send(
                        features.at[:, columns(target, chunk)],
                        inbox.at[chunk, blocks + me],
                        send_in,
                        recv_in.at[chunk],
                        {"ctx": target},
                    )

        pltpu.make_async_copy(
            features.at[:, columns(me, chunk)], inbox.at[chunk, blocks + me], recv_in.at[chunk]
        ).start()
        return carry

    lax.fori_loop(0, chunks, send_chunk, 0)
    fetch_taps.wait()
    fetch_filters.wait()

    row_index = lax.broadcasted_iota(jnp.int32, (rows, rows), 0)
    lane_index = lax.broadcasted_iota(jnp.int32, (rows, rows), 1)
    upper = lane_index >= row_index
    lane_group = lane_index // group
    zero_tile = jnp.zeros((rows, rows), jnp.float32)

    def convolve(tap_rows, feat_at, grad_at, kernel_at, feat_blocks, grad_blocks):
        for block in range(feat_blocks):
            wide_feat[8 + block * rows : 8 + (block + 1) * rows, :] = feat_at(block).astype(
                jnp.float32
            )
        for block in range(feat_blocks):
            here = slice(block * rows, (block + 1) * rows)
            summed = zero_tile
            for tap in range(taps_count):
                start = 8 + block * rows - tap
                summed = summed + tap_rows[tap] * wide_feat[start : start + rows, :]
            high = summed.astype(jnp.bfloat16)
            low = (summed - high.astype(jnp.float32)).astype(jnp.bfloat16)
            split_in[here, 0:width] = high
            split_in[here, width : 2 * width] = low
        for block in range(grad_blocks):
            here = slice(block * rows, (block + 1) * rows)
            grad = grad_at(block)
            twin_grad[here, 0:width] = grad
            twin_grad[here, width : 2 * width] = grad
            pair_grad[here, 0:width] = grad
            if block:
                pair_grad[(block - 1) * rows : block * rows, width : 2 * width] = grad
        pair_grad[(grad_blocks - 1) * rows : grad_blocks * rows, width : 2 * width] = jnp.zeros(
            (rows, width), jnp.bfloat16
        )

        def do_filter(index, inner):
            ours = lane_group == index
            kernel_row = kernel_at(index)
            highs, lows = [], []
            last = zero_tile
            for block in range(grad_blocks):
                spread = jnp.broadcast_to(
                    kernel_row[:, block * rows : (block + 1) * rows], (rows, rows)
                )
                rolled = pltpu.roll(spread, 0, 1, stride=1, stride_axis=0)
                tile = jnp.where(upper, rolled, last)
                last = rolled
                high = tile.astype(jnp.bfloat16)
                highs.append(high)
                lows.append((tile - high.astype(jnp.float32)).astype(jnp.bfloat16))
            table = jnp.concatenate(
                [jnp.concatenate(highs, axis=1), jnp.concatenate(lows, axis=1)], axis=0
            )
            for block in range(0, feat_blocks, 2):
                product = jnp.dot(
                    table[:, : (grad_blocks - block) * rows],
                    pair_grad[block * rows : grad_blocks * rows, :],
                    preferred_element_type=jnp.float32,
                )
                both = product[:rows] + product[rows:]
                for side in range(2):
                    here = slice((block + side) * rows, (block + side + 1) * rows)
                    conv_grad[here, :] = jnp.where(
                        ours, both[:, side * width : (side + 1) * width], conv_grad[here, :]
                    )
            ours_twice = jnp.concatenate([ours, ours], axis=1)
            picked = [
                jnp.where(
                    ours_twice,
                    split_in[block * rows : (block + 1) * rows, :],
                    jnp.zeros((rows, 2 * width), jnp.bfloat16),
                )
                for block in range(feat_blocks)
            ]
            sums = [None] * grad_blocks
            for block in range(0, grad_blocks, 2):
                product = lax.dot_general(
                    jnp.concatenate(picked[: block + 2], axis=0),
                    twin_grad[block * rows : (block + 2) * rows, :],
                    (((1,), (1,)), ((), ())),
                    preferred_element_type=jnp.float32,
                )
                for side in range(2):
                    for early in range(min(feat_blocks, block + side + 1)):
                        lag = block + side - early
                        piece = product[
                            early * rows : (early + 1) * rows, side * rows : (side + 1) * rows
                        ]
                        sums[lag] = piece if sums[lag] is None else sums[lag] + piece
            for lag in range(grad_blocks):
                following = sums[lag + 1] if lag + 1 < grad_blocks else zero_tile
                merged = jnp.where(upper, sums[lag], following)
                folded = merged[0:8]
                for part in range(1, rows // 8):
                    folded = folded + pltpu.roll(
                        merged[part * 8 : part * 8 + 8], rows - part * 8, 1
                    )
                place = pl.multiple_of((lag * per_chunk + index) * 8, 8)
                diagonals[pl.ds(place, 8), :] = folded
            return inner

        lax.fori_loop(0, per_chunk, do_filter, 0)
        count = grad_blocks * per_chunk
        lagged = diagonals[pl.ds(0, count, stride=8), :]
        for turn in range(1, 8):
            lagged = lagged + pltpu.roll(
                diagonals[pl.ds(turn, count, stride=8), :], rows - turn, 1
            )
        return [
            lagged[lag * per_chunk : (lag + 1) * per_chunk] for lag in range(grad_blocks)
        ]

    def finish(tap_rows, feat_blocks, put):
        tap_sums = [jnp.zeros((1, width), jnp.float32)] * taps_count
        for block in range(feat_blocks):
            here = block * rows
            summed = zero_tile
            grads = conv_grad[here : here + rows, :]
            for tap in range(taps_count):
                summed = (
                    summed + tap_rows[tap] * conv_grad[here + tap : here + tap + rows, :]
                )
                start = 8 + here - tap
                tap_sums[tap] = tap_sums[tap] + jnp.sum(
                    grads * wide_feat[start : start + rows, :], axis=0, keepdims=True
                )
            put(block, summed.astype(jnp.bfloat16))
        if per_chunk > taps_count:
            tap_sums.append(jnp.zeros((per_chunk - taps_count, width), jnp.float32))
        return jnp.concatenate(tap_sums, axis=0)

    edge_zero = jnp.zeros((8, width), jnp.float32)

    def put_out(chunk):
        def put(block, value):
            outbox[chunk, block] = value

        return put

    def keep_shares(chunk, lags, tap_share):
        for lag in range(blocks):
            shares[dp_rank, chunk, :, lag * rows : (lag + 1) * rows] = lags[lag]
        shares[dp_rank, chunk, :, seq_len : seq_len + width] = tap_share

    def send_shares(chunk):
        for step in range(1, dp_count):
            send(
                shares.at[dp_rank, chunk],
                shares.at[dp_rank, chunk],
                send_share,
                recv_share,
                {"dp": lax.rem(dp_rank + step, dp_count)},
            )

    def own_columns(chunk):
        return feature_out.at[:, columns(me, chunk)]

    def do_early(chunk, carry):
        landed = inbox.at[chunk, 0 : blocks + half]
        pltpu.make_async_copy(landed, landed, recv_in.at[chunk]).wait()
        tap_rows = tap_rows_of(me, chunk)
        wide_feat[0:8, :] = edge_zero
        lags = convolve(
            tap_rows,
            lambda block: inbox[chunk, blocks + block],
            lambda block: inbox[chunk, block],
            lambda index: filters[pl.ds(chunk * per_chunk + index, 1), :],
            half,
            blocks,
        )
        bundle = late_landed.at[chunk]
        pltpu.make_async_copy(bundle, bundle, recv_landed.at[chunk]).wait()
        lent = half * rows
        conv_grad[lent : lent + 8, :] = late_landed[chunk, :, lent + width : lent + 2 * width]
        tap_share = finish(tap_rows, half, put_out(chunk))
        tap_share = tap_share + late_landed[chunk, :, lent : lent + width]
        for lag in range(half):
            lags[lag] = lags[lag] + late_landed[chunk, :, lag * rows : (lag + 1) * rows]
        keep_shares(chunk, lags, tap_share)
        other = half - 1 - me
        send(outbox.at[chunk, other], own_columns(chunk), send_out, recv_out, {"ctx": other})
        pltpu.make_async_copy(outbox.at[chunk, me], own_columns(chunk), recv_out).start()
        send_shares(chunk)
        return carry

    def do_late(chunk, carry):
        owner = me - half
        landed = late_inbox.at[chunk]
        pltpu.make_async_copy(landed, landed, recv_late.at[chunk]).wait()
        edge = late_edge.at[chunk]
        pltpu.make_async_copy(edge, edge, recv_edge.at[chunk]).wait()
        lent_here = lent_filters.at[chunk]
        pltpu.make_async_copy(lent_here, lent_here, recv_lent.at[chunk]).wait()
        tap_rows = tap_rows_of(owner, chunk)
        wide_feat[0:8, :] = late_edge[chunk].astype(jnp.float32)[8:16]
        lags = convolve(
            tap_rows,
            lambda block: late_inbox[chunk, half + block],
            lambda block: late_inbox[chunk, block],
            lambda index: lent_filters[chunk, pl.ds(index, 1), :],
            half,
            half,
        )
        conv_grad[half * rows : half * rows + 8, :] = edge_zero

        def put(block, value):
            late_outbox[chunk, block] = value

        tap_share = finish(tap_rows, half, put)
        lent = half * rows
        for lag in range(half):
            late_share[chunk, :, lag * rows : (lag + 1) * rows] = lags[lag]
        late_share[chunk, :, lent : lent + width] = tap_share
        late_share[chunk, :, lent + width : lent + 2 * width] = conv_grad[0:8, :]
        send(
            late_share.at[chunk],
            late_landed.at[chunk],
            send_late,
            recv_landed.at[chunk],
            {"ctx": owner},
        )
        place = feature_out.at[:, columns(owner, chunk)]
        other = half - 1 - owner
        send(late_outbox.at[chunk, other], place, send_out, recv_out, {"ctx": half + other})
        pltpu.make_async_copy(late_outbox.at[chunk, owner], place, recv_out).start()

        landed = inbox.at[chunk]
        pltpu.make_async_copy(landed, landed, recv_in.at[chunk]).wait()
        tap_rows = tap_rows_of(me, chunk)
        wide_feat[0:8, :] = edge_zero
        lags = convolve(
            tap_rows,
            lambda block: inbox[chunk, blocks + block],
            lambda block: inbox[chunk, block],
            lambda index: filters[pl.ds(chunk * per_chunk + index, 1), :],
            blocks,
            blocks,
        )
        conv_grad[seq_len : seq_len + 8, :] = edge_zero
        tap_share = finish(tap_rows, blocks, put_out(chunk))
        keep_shares(chunk, lags, tap_share)
        for step in range(1, blocks):
            target = lax.rem(me + step, blocks)
            send(
                outbox.at[chunk, target], own_columns(chunk), send_out, recv_out, {"ctx": target}
            )
        pltpu.make_async_copy(outbox.at[chunk, me], own_columns(chunk), recv_out).start()
        send_shares(chunk)
        return carry

    def drain(ref, sem):
        pltpu.make_async_copy(ref, ref, sem).wait()

    @pl.when(is_early)
    def _():
        lax.fori_loop(0, chunks, do_early, 0)

    @pl.when(is_late)
    def _():
        lax.fori_loop(0, chunks, do_late, 0)

    drain(shares.at[0 : dp_count - 1], recv_share)
    filter_scale = 1.0 / math.sqrt(dp_count * group * seq_len)
    tap_scale = 1.0 / math.sqrt(dp_count * seq_len)
    for chunk in range(chunks):
        total = shares[0, chunk]
        for rank in range(1, dp_count):
            total = total + shares[rank, chunk]
        filter_out[chunk * per_chunk : (chunk + 1) * per_chunk, :] = (
            total[:, :seq_len] * filter_scale
        )
        tap_out[:, chunk * width : (chunk + 1) * width] = total[:taps_count, seq_len:] * tap_scale
    drain(shares.at[0 : dp_count - 1], send_share)

    @pl.when(is_early)
    def _():
        drain(lent_filters, send_lent)
        drain(inbox.at[:, 0 : 2 * blocks - 1], send_in)
        drain(outbox.at[:, 0 : half - 1], send_out)

    @pl.when(me == half - 1)
    def _():
        for _ in range(half):
            drain(late_edge, send_edge)

    @pl.when(is_late)
    def _():
        drain(inbox, send_in)
        drain(outbox, send_out)
        drain(late_share, send_late)

    drain(outbox, recv_out)


def fused_body(arriving, features, short_taps, filters):
    blocks = lax.axis_size("ctx")
    dp_count = lax.axis_size("dp")
    pipe_count = lax.axis_size("pipe")
    rows, channels = features.shape[2], features.shape[3]
    own_width = channels // blocks
    filter_count, seq_len = filters.shape[1], filters.shape[2]
    group = own_width // filter_count
    taps_count = short_taps.shape[1]
    width = rows
    half = blocks // 2
    chunks = own_width // width
    per_chunk = width // group
    lent = half * rows
    sizes = (blocks, dp_count, pipe_count, chunks, rows, width, group, taps_count)
    anywhere = pl.BlockSpec(memory_space=pltpu.HBM)
    vmem = pl.BlockSpec(memory_space=pltpu.VMEM)
    one_sem = pltpu.SemaphoreType.DMA
    chunk_sems = pltpu.SemaphoreType.DMA((chunks,))
    feature_grads, filter_grads, tap_grads = pl.pallas_call(
        functools.partial(fused_kernel, sizes),
        out_shape=(
            jax.ShapeDtypeStruct((rows, channels), jnp.bfloat16),
            jax.ShapeDtypeStruct((filter_count, seq_len), jnp.float32),
            jax.ShapeDtypeStruct((taps_count, own_width), jnp.float32),
        ),
        in_specs=[anywhere] * 4,
        out_specs=(anywhere, vmem, vmem),
        scratch_shapes=[
            pltpu.VMEM((taps_count, channels // width, width), jnp.float32),
            pltpu.VMEM((filter_count, seq_len), jnp.float32),
            pltpu.VMEM((chunks, per_chunk, lent), jnp.float32),
            pltpu.VMEM((chunks, 2 * blocks, rows, width), jnp.bfloat16),
            pltpu.VMEM((chunks, 2 * half, rows, width), jnp.bfloat16),
            pltpu.VMEM((chunks, 16, width), jnp.bfloat16),
            pltpu.VMEM((chunks, blocks, rows, width), jnp.bfloat16),
            pltpu.VMEM((chunks, half, rows, width), jnp.bfloat16),
            pltpu.VMEM((dp_count, chunks, per_chunk, seq_len + width), jnp.float32),
            pltpu.VMEM((chunks, per_chunk, lent + 2 * width), jnp.float32),
            pltpu.VMEM((chunks, per_chunk, lent + 2 * width), jnp.float32),
            pltpu.VMEM((seq_len + 8, width), jnp.float32),
            pltpu.VMEM((seq_len, 2 * width), jnp.bfloat16),
            pltpu.VMEM((seq_len, 2 * width), jnp.bfloat16),
            pltpu.VMEM((seq_len, 2 * width), jnp.bfloat16),
            pltpu.VMEM((seq_len + 8, width), jnp.float32),
            pltpu.VMEM((blocks * per_chunk * 8, width), jnp.float32),
            pltpu.SemaphoreType.DMA((2,)),
            one_sem,
            chunk_sems,
            chunk_sems,
            one_sem,
            chunk_sems,
            one_sem,
            chunk_sems,
            one_sem,
            chunk_sems,
            one_sem,
            one_sem,
            one_sem,
            one_sem,
        ],
        compiler_params=pltpu.CompilerParams(
            collective_id=0, has_side_effects=True, vmem_limit_bytes=60 * 1024 * 1024
        ),
    )(
        arriving[0, 0],
        features[0, 0],
        short_taps.reshape(taps_count, channels // width, width),
        filters,
    )
    return (feature_grads[None, None], filter_grads[None], tap_grads[None])


def fits_fused(mesh, features, short_taps, filters):
    blocks, rows = mesh.shape["ctx"], features.shape[2] // mesh.shape["ctx"]
    own_width = features.shape[3] // blocks
    own_filters = filters.shape[1] // blocks
    group = own_width // own_filters
    return (
        rows == 128
        and blocks == 4
        and mesh.shape["pipe"] == 2
        and own_width % rows == 0
        and rows % group == 0
        and rows // group == 8
        and short_taps.shape[1] <= 8
    )


def solution(mesh):
    in_specs = (
        P("pipe", "dp", "ctx", None),
        P("pipe", "dp", "ctx", None),
        P("pipe", None, None),
        P("pipe", "ctx", None),
    )
    out_specs = (P("pipe", "dp", "ctx", None), P("pipe", "ctx", None), P("pipe", None, "ctx"))

    def run(arriving, features, short_taps, filters):
        chosen = fused_body if fits_fused(mesh, features, short_taps, filters) else body
        return jax.shard_map(
            chosen, mesh=mesh, in_specs=in_specs, out_specs=out_specs, check_vma=False
        )(arriving, features, short_taps, filters)

    return run
```

```python
import functools
import math

import jax
import jax.numpy as jnp
from jax import lax
from jax.experimental import pallas as pl
from jax.experimental.pallas import tpu as pltpu
from jax.sharding import PartitionSpec as P

TABLE_PRECISION = lax.Precision.HIGH
MESH = pl.DeviceIdType.MESH


def passed_along(value, axis, steps):
    count = lax.axis_size(axis)
    pairs = [(source, (source + steps) % count) for source in range(count)]
    return lax.ppermute(value, axis, pairs)


def phase_table(count_a, count_b, modulus):
    first_index = lax.broadcasted_iota(jnp.int32, (count_a, count_b), 0)
    second_index = lax.broadcasted_iota(jnp.int32, (count_a, count_b), 1)
    phase = (first_index * second_index % modulus).astype(jnp.float32) * (2.0 * math.pi / modulus)
    return (jnp.cos(phase), jnp.sin(phase))


def block_table(cos_part, sin_part):
    return jnp.stack(
        [
            jnp.concatenate([cos_part, -sin_part], axis=-1),
            jnp.concatenate([sin_part, cos_part], axis=-1),
        ]
    )


def split_length(seq_len):
    factor = 1
    for candidate in range(1, seq_len + 1):
        if seq_len % candidate == 0 and candidate * candidate <= 2 * seq_len:
            factor = candidate
    return factor


def finish_forward(first, inner_len, outer_len):
    full_len = inner_len * outer_len
    cos_turn, sin_turn = phase_table(inner_len, outer_len, full_len)
    first_re = first[..., :outer_len]
    first_im = first[..., outer_len:]
    turned = jnp.stack(
        [first_re * cos_turn + first_im * sin_turn, first_im * cos_turn - first_re * sin_turn],
        axis=-3,
    )
    cos_last, sin_last = phase_table(inner_len, inner_len, inner_len)
    return jnp.einsum(
        "...cnk,cne->...ke", turned, block_table(cos_last, sin_last), precision=TABLE_PRECISION
    )


def forward_pairs(values):
    inner_len = values.shape[-1]
    half_rows = values.shape[-2]
    outer_len = 2 * half_rows
    cos_first, sin_first = phase_table(half_rows, outer_len, outer_len)
    first = jnp.einsum(
        "fagmn,ame->fgne", values, block_table(cos_first, sin_first), precision=TABLE_PRECISION
    )
    return finish_forward(first, inner_len, outer_len)


def forward_real(values):
    inner_len = values.shape[-1]
    half_rows = values.shape[-2]
    outer_len = 2 * half_rows
    cos_first, sin_first = phase_table(half_rows, outer_len, outer_len)
    first = jnp.einsum(
        "fmn,me->fne", values, block_table(cos_first, sin_first)[0], precision=TABLE_PRECISION
    )
    return finish_forward(first, inner_len, outer_len)


def inverse_spectrum(spectrum, real_only):
    outer_len = spectrum.shape[-2]
    inner_len = spectrum.shape[-1] // 2
    half_rows = outer_len // 2
    full_len = outer_len * inner_len
    cos_first, sin_first = phase_table(inner_len, inner_len, inner_len)
    table_first = jnp.concatenate(
        [
            jnp.concatenate([cos_first, sin_first], axis=1),
            jnp.concatenate([-sin_first, cos_first], axis=1),
        ],
        axis=0,
    )
    step = jnp.einsum("...ke,ew->...kw", spectrum, table_first, precision=TABLE_PRECISION)
    step_re = step[..., :inner_len]
    step_im = step[..., inner_len:]
    cos_turn, sin_turn = phase_table(outer_len, inner_len, full_len)
    turned = jnp.stack(
        [step_re * cos_turn - step_im * sin_turn, step_re * sin_turn + step_im * cos_turn], axis=-3
    )
    cos_last, sin_last = phase_table(half_rows, outer_len, outer_len)
    table_last = jnp.stack(
        [jnp.stack([cos_last, -sin_last], axis=1), jnp.stack([sin_last, cos_last], axis=1)]
    )
    norm_factor = 1.0 / full_len
    if real_only:
        return (
            jnp.einsum("mck,...ckn->m...n", table_last[0], turned, precision=TABLE_PRECISION)
            * norm_factor
        )
    return (
        jnp.einsum("dmck,...ckn->dm...n", table_last, turned, precision=TABLE_PRECISION)
        * norm_factor
    )


def body(arriving, features, short_taps, filters):
    ctx_count = lax.axis_size("ctx")
    ctx_rank = lax.axis_index("ctx")
    dp_count = lax.axis_size("dp")
    rows_dev = features.shape[2]
    channels = features.shape[3]
    own_width = channels // ctx_count
    filter_count = filters.shape[1]
    group_size = own_width // filter_count
    half_group = group_size // 2
    taps_count = short_taps.shape[1]
    seq_len = filters.shape[2]
    inner_len = split_length(seq_len)
    half_rows = seq_len // inner_len
    feature_cols = features[0, 0].T
    arrived = passed_along(arriving, "pipe", -1)
    gradient_cols = arrived[0, 0].T
    gradient_block, feature_block = (
        lax.all_to_all(gradient_cols, "ctx", split_axis=0, concat_axis=1, tiled=True),
        lax.all_to_all(feature_cols, "ctx", split_axis=0, concat_axis=1, tiled=True),
    )
    tap_block = lax.dynamic_slice_in_dim(short_taps[0], ctx_rank * own_width, own_width, 1)
    feature_vals = feature_block.astype(jnp.float32)
    padded_feat = jnp.pad(feature_vals, ((0, 0), (taps_count - 1, 0)))
    conv_in = jnp.zeros(feature_vals.shape, jnp.float32)
    for offset in range(taps_count):
        conv_in = (
            conv_in
            + tap_block[offset][:, None]
            * padded_feat[:, taps_count - 1 - offset : taps_count - 1 - offset + seq_len]
        )
    pair_shape = (filter_count, 2, half_group, half_rows, inner_len)
    spectrum_u = forward_pairs(conv_in.reshape(pair_shape))
    spectrum_g = forward_pairs(gradient_block.astype(jnp.float32).reshape(pair_shape))
    spectrum_h = forward_real(filters[0].reshape(filter_count, half_rows, inner_len))[:, None]
    g_re = spectrum_g[..., :inner_len]
    g_im = spectrum_g[..., inner_len:]
    u_re = spectrum_u[..., :inner_len]
    u_im = spectrum_u[..., inner_len:]
    h_re = spectrum_h[..., :inner_len]
    h_im = spectrum_h[..., inner_len:]
    back = jnp.concatenate([h_re * g_re + h_im * g_im, h_re * g_im - h_im * g_re], axis=-1)
    lag = jnp.concatenate(
        [jnp.sum(g_re * u_re + g_im * u_im, axis=1), jnp.sum(g_im * u_re - g_re * u_im, axis=1)],
        axis=-1,
    )
    grad_blocks = inverse_spectrum(back, False)
    conv_in_grad = jnp.transpose(grad_blocks, (2, 0, 3, 1, 4)).reshape(own_width, seq_len)
    filter_part = jnp.transpose(inverse_spectrum(lag, True), (1, 0, 2)).reshape(
        filter_count, seq_len
    )
    padded_grad = jnp.pad(conv_in_grad, ((0, 0), (0, taps_count - 1)))
    feature_grad = jnp.zeros(conv_in_grad.shape, jnp.float32)
    tap_terms = []
    for offset in range(taps_count):
        feature_grad = (
            feature_grad + tap_block[offset][:, None] * padded_grad[:, offset : offset + seq_len]
        )
        tap_terms.append(
            jnp.sum(
                conv_in_grad
                * padded_feat[:, taps_count - 1 - offset : taps_count - 1 - offset + seq_len],
                axis=1,
            )
        )
    tap_part = jnp.stack(tap_terms)
    filter_total, tap_total = lax.psum((filter_part, tap_part), "dp")
    back_cols = feature_grad.astype(jnp.bfloat16)
    feature_rows = lax.all_to_all(back_cols, "ctx", split_axis=1, concat_axis=0, tiled=True)
    feature_grads = feature_rows.T.reshape(1, 1, rows_dev, channels)
    filter_scale = 1.0 / math.sqrt(dp_count * group_size * seq_len)
    tap_scale = 1.0 / math.sqrt(dp_count * seq_len)
    filter_grads = (filter_total * filter_scale)[None]
    tap_grads = (tap_total * tap_scale).reshape(1, taps_count, own_width)
    return (feature_grads, filter_grads, tap_grads)


def fused_kernel(
    sizes,
    arriving,
    features,
    taps_all,
    filters_all,
    feature_out,
    filter_out,
    tap_out,
    taps,
    filters,
    lent_filters,
    inbox,
    late_inbox,
    late_edge,
    outbox,
    late_outbox,
    shares,
    late_share,
    late_landed,
    wide_feat,
    split_in,
    grad_cols,
    turned,
    conv_cols,
    conv_grad,
    diagonals,
    local_sems,
    send_in,
    recv_in,
    recv_late,
    send_edge,
    recv_edge,
    send_lent,
    recv_lent,
    send_late,
    recv_landed,
    send_out,
    recv_out,
    send_share,
    recv_share,
):
    blocks, dp_count, pipe_count, chunks, rows, width, group, taps_count = sizes
    seq_len = blocks * rows
    half = blocks // 2
    own_width = chunks * width
    per_chunk = width // group
    me = lax.axis_index("ctx")
    dp_rank = lax.axis_index("dp")
    pipe_rank = lax.axis_index("pipe")
    before = lax.rem(pipe_rank + pipe_count - 1, pipe_count)
    is_early = me < half
    is_late = me >= half

    fetch_taps = pltpu.make_async_copy(taps_all, taps, local_sems.at[0])
    fetch_taps.start()
    fetch_filters = pltpu.make_async_copy(filters_all.at[0], filters, local_sems.at[1])
    fetch_filters.start()

    barrier = pltpu.get_barrier_semaphore()
    for step in range(1, blocks):
        pl.semaphore_signal(
            barrier,
            inc=1,
            device_id={"ctx": lax.rem(me + step, blocks)},
            device_id_type=MESH,
        )
    for step in range(blocks):
        pl.semaphore_signal(
            barrier,
            inc=1,
            device_id={"pipe": before, "ctx": lax.rem(me + step, blocks)},
            device_id_type=MESH,
        )
    for step in range(1, dp_count):
        pl.semaphore_signal(
            barrier,
            inc=1,
            device_id={"dp": lax.rem(dp_rank + step, dp_count)},
            device_id_type=MESH,
        )
    pl.semaphore_wait(barrier, 2 * blocks + dp_count - 2)

    def columns(owner, chunk):
        return pl.ds(pl.multiple_of(owner * own_width + chunk * width, width), width)

    def tap_rows_of(owner, chunk):
        place = owner * chunks + chunk
        return [taps[tap, pl.ds(place, 1), :] for tap in range(taps_count)]

    def send(source, target, send_sem, recv_sem, device):
        pltpu.make_async_remote_copy(
            src_ref=source,
            dst_ref=target,
            send_sem=send_sem,
            recv_sem=recv_sem,
            device_id=device,
            device_id_type=MESH,
        ).start()

    def send_chunk(chunk, carry):
        @pl.when(is_early)
        def _():
            send(
                filters_all.at[0, pl.ds(pl.multiple_of(chunk * per_chunk, 8), per_chunk), 0 : half * rows],
                lent_filters.at[chunk],
                send_lent,
                recv_lent.at[chunk],
                {"ctx": me + half},
            )

        @pl.when(me == half - 1)
        def _():
            for owner in range(half):
                send(
                    features.at[rows - 16 : rows, columns(owner, chunk)],
                    late_edge.at[chunk],
                    send_edge,
                    recv_edge.at[chunk],
                    {"ctx": half + owner},
                )

        @pl.when(is_late)
        def _():
            for step in range(half):
                owner = lax.rem(me + step, half)
                device = owner + half
                send(
                    arriving.at[:, columns(owner, chunk)],
                    late_inbox.at[chunk, me - half],
                    send_in,
                    recv_late.at[chunk],
                    {"pipe": before, "ctx": device},
                )
                if step:
                    send(
                        features.at[:, columns(owner, chunk)],
                        late_inbox.at[chunk, me],
                        send_in,
                        recv_late.at[chunk],
                        {"ctx": device},
                    )
                else:
                    pltpu.make_async_copy(
                        features.at[:, columns(owner, chunk)],
                        late_inbox.at[chunk, me],
                        recv_late.at[chunk],
                    ).start()

        for step in range(blocks):
            target = lax.rem(me + step, blocks)
            send(
                arriving.at[:, columns(target, chunk)],
                inbox.at[chunk, me],
                send_in,
                recv_in.at[chunk],
                {"pipe": before, "ctx": target},
            )
            if step:

                @pl.when(jnp.logical_or(is_early, target >= half))
                def _():
                    send(
                        features.at[:, columns(target, chunk)],
                        inbox.at[chunk, blocks + me],
                        send_in,
                        recv_in.at[chunk],
                        {"ctx": target},
                    )

        pltpu.make_async_copy(
            features.at[:, columns(me, chunk)], inbox.at[chunk, blocks + me], recv_in.at[chunk]
        ).start()
        return carry

    lax.fori_loop(0, chunks, send_chunk, 0)
    fetch_taps.wait()
    fetch_filters.wait()

    row_index = lax.broadcasted_iota(jnp.int32, (rows, rows), 0)
    lane_index = lax.broadcasted_iota(jnp.int32, (rows, rows), 1)
    upper = lane_index >= row_index
    lower = row_index >= lane_index
    mirror = (lax.rem(row_index + lane_index, rows) == 0).astype(jnp.bfloat16)
    zero_tile = jnp.zeros((rows, rows), jnp.float32)

    def convolve(tap_rows, feat_at, grad_at, kernel_rows, feat_blocks, grad_blocks):
        for block in range(feat_blocks):
            wide_feat[8 + block * rows : 8 + (block + 1) * rows, :] = feat_at(block).astype(
                jnp.float32
            )
        for block in range(feat_blocks):
            here = slice(block * rows, (block + 1) * rows)
            summed = zero_tile
            for tap in range(taps_count):
                start = 8 + block * rows - tap
                summed = summed + tap_rows[tap] * wide_feat[start : start + rows, :]
            summed = summed.T
            high = summed.astype(jnp.bfloat16)
            split_in[0, :, here] = high
            split_in[1, :, here] = (summed - high.astype(jnp.float32)).astype(jnp.bfloat16)
        for block in range(grad_blocks):
            grad_cols[:, block * rows : (block + 1) * rows] = grad_at(block).T
        grad_cols[:, grad_blocks * rows : (grad_blocks + feat_blocks - 1) * rows] = jnp.zeros(
            (width, (feat_blocks - 1) * rows), jnp.bfloat16
        )
        for block in range(grad_blocks):
            here = slice(block * rows, (block + 1) * rows)
            whole = kernel_rows[:, here]
            high = whole.astype(jnp.bfloat16)
            low = (whole - high.astype(jnp.float32)).astype(jnp.bfloat16)
            turned[:, here] = jnp.dot(
                high, mirror, preferred_element_type=jnp.float32
            ) + jnp.dot(low, mirror, preferred_element_type=jnp.float32)

        def one_filter(index):
            ours = pl.ds(pl.multiple_of(index * group, group), group)
            kernel_row = turned[pl.ds(index, 1), :]
            highs, lows = [], []
            last = zero_tile
            for block in range(grad_blocks):
                spread = jnp.broadcast_to(
                    kernel_row[:, block * rows : (block + 1) * rows], (rows, rows)
                )
                rolled = pltpu.roll(spread, 0, 1, stride=1, stride_axis=0)
                tile = jnp.where(lower, rolled, last)
                last = rolled
                high = tile.astype(jnp.bfloat16)
                highs.append(high)
                lows.append((tile - high.astype(jnp.float32)).astype(jnp.bfloat16))
            table = jnp.concatenate(
                [jnp.concatenate(highs, axis=0), jnp.concatenate(lows, axis=0)], axis=1
            )
            shifted = jnp.concatenate(
                [
                    grad_cols[ours, block * rows : (block + grad_blocks) * rows]
                    for block in range(feat_blocks)
                ],
                axis=0,
            )
            product = jnp.dot(shifted, table, preferred_element_type=jnp.float32)
            both = product[:, :rows] + product[:, rows:]
            for block in range(feat_blocks):
                conv_cols[ours, block * rows : (block + 1) * rows] = both[
                    block * group : (block + 1) * group
                ]
            picked = jnp.concatenate(
                [
                    split_in[part, ours, block * rows : (block + 1) * rows]
                    for part in range(2)
                    for block in range(feat_blocks)
                ],
                axis=0,
            )
            sums = jnp.dot(
                picked.T,
                jnp.concatenate([shifted, shifted], axis=0),
                preferred_element_type=jnp.float32,
            )
            for lag in range(grad_blocks):
                following = (
                    sums[:, (lag + 1) * rows : (lag + 2) * rows]
                    if lag + 1 < grad_blocks
                    else zero_tile
                )
                merged = jnp.where(upper, sums[:, lag * rows : (lag + 1) * rows], following)
                folded = [merged[0:8]]
                for part in range(1, rows // 8):
                    folded.append(
                        pltpu.roll(merged[part * 8 : part * 8 + 8], rows - part * 8, 1)
                    )
                while len(folded) > 1:
                    folded = [
                        folded[place] + folded[place + 1] for place in range(0, len(folded), 2)
                    ]
                place = pl.multiple_of((lag * per_chunk + index) * 8, 8)
                diagonals[pl.ds(place, 8), :] = folded[0]

        def do_filters(index, inner):
            one_filter(2 * index)
            one_filter(2 * index + 1)
            return inner

        lax.fori_loop(0, per_chunk // 2, do_filters, 0)
        for block in range(feat_blocks):
            here = slice(block * rows, (block + 1) * rows)
            conv_grad[here, :] = conv_cols[:, here].T
        count = grad_blocks * per_chunk
        lagged = diagonals[pl.ds(0, count, stride=8), :]
        for turn in range(1, 8):
            lagged = lagged + pltpu.roll(
                diagonals[pl.ds(turn, count, stride=8), :], rows - turn, 1
            )
        return [
            lagged[lag * per_chunk : (lag + 1) * per_chunk] for lag in range(grad_blocks)
        ]

    def finish(tap_rows, feat_blocks, put):
        tap_sums = [jnp.zeros((1, width), jnp.float32)] * taps_count
        for block in range(feat_blocks):
            here = block * rows
            summed = zero_tile
            grads = conv_grad[here : here + rows, :]
            for tap in range(taps_count):
                summed = (
                    summed + tap_rows[tap] * conv_grad[here + tap : here + tap + rows, :]
                )
                start = 8 + here - tap
                tap_sums[tap] = tap_sums[tap] + jnp.sum(
                    grads * wide_feat[start : start + rows, :], axis=0, keepdims=True
                )
            put(block, summed.astype(jnp.bfloat16))
        if per_chunk > taps_count:
            tap_sums.append(jnp.zeros((per_chunk - taps_count, width), jnp.float32))
        return jnp.concatenate(tap_sums, axis=0)

    edge_zero = jnp.zeros((8, width), jnp.float32)

    def put_out(chunk):
        def put(block, value):
            outbox[chunk, block] = value

        return put

    def keep_shares(chunk, lags, tap_share):
        for lag in range(blocks):
            shares[dp_rank, chunk, :, lag * rows : (lag + 1) * rows] = lags[lag]
        shares[dp_rank, chunk, :, seq_len : seq_len + width] = tap_share

    def send_shares(chunk):
        for step in range(1, dp_count):
            send(
                shares.at[dp_rank, chunk],
                shares.at[dp_rank, chunk],
                send_share,
                recv_share,
                {"dp": lax.rem(dp_rank + step, dp_count)},
            )

    def own_columns(chunk):
        return feature_out.at[:, columns(me, chunk)]

    def do_early(chunk, carry):
        landed = inbox.at[chunk, 0 : blocks + half]
        pltpu.make_async_copy(landed, landed, recv_in.at[chunk]).wait()
        tap_rows = tap_rows_of(me, chunk)
        wide_feat[0:8, :] = edge_zero
        lags = convolve(
            tap_rows,
            lambda block: inbox[chunk, blocks + block],
            lambda block: inbox[chunk, block],
            filters[pl.ds(pl.multiple_of(chunk * per_chunk, 8), per_chunk), :],
            half,
            blocks,
        )
        bundle = late_landed.at[chunk]
        pltpu.make_async_copy(bundle, bundle, recv_landed.at[chunk]).wait()
        lent = half * rows
        conv_grad[lent : lent + 8, :] = late_landed[chunk, :, lent + width : lent + 2 * width]
        tap_share = finish(tap_rows, half, put_out(chunk))
        tap_share = tap_share + late_landed[chunk, :, lent : lent + width]
        for lag in range(half):
            lags[lag] = lags[lag] + late_landed[chunk, :, lag * rows : (lag + 1) * rows]
        keep_shares(chunk, lags, tap_share)
        other = half - 1 - me
        send(outbox.at[chunk, other], own_columns(chunk), send_out, recv_out, {"ctx": other})
        pltpu.make_async_copy(outbox.at[chunk, me], own_columns(chunk), recv_out).start()
        send_shares(chunk)
        return carry

    def do_late(chunk, carry):
        owner = me - half
        landed = late_inbox.at[chunk]
        pltpu.make_async_copy(landed, landed, recv_late.at[chunk]).wait()
        edge = late_edge.at[chunk]
        pltpu.make_async_copy(edge, edge, recv_edge.at[chunk]).wait()
        lent_here = lent_filters.at[chunk]
        pltpu.make_async_copy(lent_here, lent_here, recv_lent.at[chunk]).wait()
        tap_rows = tap_rows_of(owner, chunk)
        wide_feat[0:8, :] = late_edge[chunk].astype(jnp.float32)[8:16]
        lags = convolve(
            tap_rows,
            lambda block: late_inbox[chunk, half + block],
            lambda block: late_inbox[chunk, block],
            lent_filters[chunk],
            half,
            half,
        )
        conv_grad[half * rows : half * rows + 8, :] = edge_zero

        def put(block, value):
            late_outbox[chunk, block] = value

        tap_share = finish(tap_rows, half, put)
        lent = half * rows
        for lag in range(half):
            late_share[chunk, :, lag * rows : (lag + 1) * rows] = lags[lag]
        late_share[chunk, :, lent : lent + width] = tap_share
        late_share[chunk, :, lent + width : lent + 2 * width] = conv_grad[0:8, :]
        send(
            late_share.at[chunk],
            late_landed.at[chunk],
            send_late,
            recv_landed.at[chunk],
            {"ctx": owner},
        )
        place = feature_out.at[:, columns(owner, chunk)]
        other = half - 1 - owner
        send(late_outbox.at[chunk, other], place, send_out, recv_out, {"ctx": half + other})
        pltpu.make_async_copy(late_outbox.at[chunk, owner], place, recv_out).start()

        landed = inbox.at[chunk]
        pltpu.make_async_copy(landed, landed, recv_in.at[chunk]).wait()
        tap_rows = tap_rows_of(me, chunk)
        wide_feat[0:8, :] = edge_zero
        lags = convolve(
            tap_rows,
            lambda block: inbox[chunk, blocks + block],
            lambda block: inbox[chunk, block],
            filters[pl.ds(pl.multiple_of(chunk * per_chunk, 8), per_chunk), :],
            blocks,
            blocks,
        )
        conv_grad[seq_len : seq_len + 8, :] = edge_zero
        tap_share = finish(tap_rows, blocks, put_out(chunk))
        keep_shares(chunk, lags, tap_share)
        for step in range(1, blocks):
            target = lax.rem(me + step, blocks)
            send(
                outbox.at[chunk, target], own_columns(chunk), send_out, recv_out, {"ctx": target}
            )
        pltpu.make_async_copy(outbox.at[chunk, me], own_columns(chunk), recv_out).start()
        send_shares(chunk)
        return carry

    def drain(ref, sem):
        pltpu.make_async_copy(ref, ref, sem).wait()

    @pl.when(is_early)
    def _():
        lax.fori_loop(0, chunks, do_early, 0)

    @pl.when(is_late)
    def _():
        lax.fori_loop(0, chunks, do_late, 0)

    drain(shares.at[0 : dp_count - 1], recv_share)
    filter_scale = 1.0 / math.sqrt(dp_count * group * seq_len)
    tap_scale = 1.0 / math.sqrt(dp_count * seq_len)
    for chunk in range(chunks):
        total = shares[0, chunk]
        for rank in range(1, dp_count):
            total = total + shares[rank, chunk]
        filter_out[chunk * per_chunk : (chunk + 1) * per_chunk, :] = (
            total[:, :seq_len] * filter_scale
        )
        tap_out[:, chunk * width : (chunk + 1) * width] = total[:taps_count, seq_len:] * tap_scale
    drain(shares.at[0 : dp_count - 1], send_share)

    @pl.when(is_early)
    def _():
        drain(lent_filters, send_lent)
        drain(inbox.at[:, 0 : 2 * blocks - 1], send_in)
        drain(outbox.at[:, 0 : half - 1], send_out)

    @pl.when(me == half - 1)
    def _():
        for _ in range(half):
            drain(late_edge, send_edge)

    @pl.when(is_late)
    def _():
        drain(inbox, send_in)
        drain(outbox, send_out)
        drain(late_share, send_late)

    drain(outbox, recv_out)


def fused_body(arriving, features, short_taps, filters):
    blocks = lax.axis_size("ctx")
    dp_count = lax.axis_size("dp")
    pipe_count = lax.axis_size("pipe")
    rows, channels = features.shape[2], features.shape[3]
    own_width = channels // blocks
    filter_count, seq_len = filters.shape[1], filters.shape[2]
    group = own_width // filter_count
    taps_count = short_taps.shape[1]
    width = rows
    half = blocks // 2
    chunks = own_width // width
    per_chunk = width // group
    lent = half * rows
    sizes = (blocks, dp_count, pipe_count, chunks, rows, width, group, taps_count)
    anywhere = pl.BlockSpec(memory_space=pltpu.HBM)
    vmem = pl.BlockSpec(memory_space=pltpu.VMEM)
    one_sem = pltpu.SemaphoreType.DMA
    chunk_sems = pltpu.SemaphoreType.DMA((chunks,))
    feature_grads, filter_grads, tap_grads = pl.pallas_call(
        functools.partial(fused_kernel, sizes),
        out_shape=(
            jax.ShapeDtypeStruct((rows, channels), jnp.bfloat16),
            jax.ShapeDtypeStruct((filter_count, seq_len), jnp.float32),
            jax.ShapeDtypeStruct((taps_count, own_width), jnp.float32),
        ),
        in_specs=[anywhere] * 4,
        out_specs=(anywhere, vmem, vmem),
        scratch_shapes=[
            pltpu.VMEM((taps_count, channels // width, width), jnp.float32),
            pltpu.VMEM((filter_count, seq_len), jnp.float32),
            pltpu.VMEM((chunks, per_chunk, lent), jnp.float32),
            pltpu.VMEM((chunks, 2 * blocks, rows, width), jnp.bfloat16),
            pltpu.VMEM((chunks, 2 * half, rows, width), jnp.bfloat16),
            pltpu.VMEM((chunks, 16, width), jnp.bfloat16),
            pltpu.VMEM((chunks, blocks, rows, width), jnp.bfloat16),
            pltpu.VMEM((chunks, half, rows, width), jnp.bfloat16),
            pltpu.VMEM((dp_count, chunks, per_chunk, seq_len + width), jnp.float32),
            pltpu.VMEM((chunks, per_chunk, lent + 2 * width), jnp.float32),
            pltpu.VMEM((chunks, per_chunk, lent + 2 * width), jnp.float32),
            pltpu.VMEM((seq_len + 8, width), jnp.float32),
            pltpu.VMEM((2, width, seq_len), jnp.bfloat16),
            pltpu.VMEM((width, 2 * seq_len), jnp.bfloat16),
            pltpu.VMEM((per_chunk, seq_len), jnp.float32),
            pltpu.VMEM((width, seq_len), jnp.float32),
            pltpu.VMEM((seq_len + 8, width), jnp.float32),
            pltpu.VMEM((blocks * per_chunk * 8, width), jnp.float32),
            pltpu.SemaphoreType.DMA((2,)),
            one_sem,
            chunk_sems,
            chunk_sems,
            one_sem,
            chunk_sems,
            one_sem,
            chunk_sems,
            one_sem,
            chunk_sems,
            one_sem,
            one_sem,
            one_sem,
            one_sem,
        ],
        compiler_params=pltpu.CompilerParams(
            collective_id=0, has_side_effects=True, vmem_limit_bytes=60 * 1024 * 1024
        ),
    )(
        arriving[0, 0],
        features[0, 0],
        short_taps.reshape(taps_count, channels // width, width),
        filters,
    )
    return (feature_grads[None, None], filter_grads[None], tap_grads[None])


def fits_fused(mesh, features, short_taps, filters):
    blocks, rows = mesh.shape["ctx"], features.shape[2] // mesh.shape["ctx"]
    own_width = features.shape[3] // blocks
    own_filters = filters.shape[1] // blocks
    group = own_width // own_filters
    return (
        rows == 128
        and blocks == 4
        and mesh.shape["pipe"] == 2
        and own_width % rows == 0
        and rows % group == 0
        and rows // group == 8
        and short_taps.shape[1] <= 8
    )


def solution(mesh):
    in_specs = (
        P("pipe", "dp", "ctx", None),
        P("pipe", "dp", "ctx", None),
        P("pipe", None, None),
        P("pipe", "ctx", None),
    )
    out_specs = (P("pipe", "dp", "ctx", None), P("pipe", "ctx", None), P("pipe", None, "ctx"))

    def run(arriving, features, short_taps, filters):
        chosen = fused_body if fits_fused(mesh, features, short_taps, filters) else body
        return jax.shard_map(
            chosen, mesh=mesh, in_specs=in_specs, out_specs=out_specs, check_vma=False
        )(arriving, features, short_taps, filters)

    return run
```

```python
import functools
import math

import jax
import jax.numpy as jnp
from jax import lax
from jax.experimental import pallas as pl
from jax.experimental.pallas import tpu as pltpu
from jax.sharding import PartitionSpec as P

TABLE_PRECISION = lax.Precision.HIGH
MESH = pl.DeviceIdType.MESH


def passed_along(value, axis, steps):
    count = lax.axis_size(axis)
    pairs = [(source, (source + steps) % count) for source in range(count)]
    return lax.ppermute(value, axis, pairs)


def phase_table(count_a, count_b, modulus):
    first_index = lax.broadcasted_iota(jnp.int32, (count_a, count_b), 0)
    second_index = lax.broadcasted_iota(jnp.int32, (count_a, count_b), 1)
    phase = (first_index * second_index % modulus).astype(jnp.float32) * (2.0 * math.pi / modulus)
    return (jnp.cos(phase), jnp.sin(phase))


def block_table(cos_part, sin_part):
    return jnp.stack(
        [
            jnp.concatenate([cos_part, -sin_part], axis=-1),
            jnp.concatenate([sin_part, cos_part], axis=-1),
        ]
    )


def split_length(seq_len):
    factor = 1
    for candidate in range(1, seq_len + 1):
        if seq_len % candidate == 0 and candidate * candidate <= 2 * seq_len:
            factor = candidate
    return factor


def finish_forward(first, inner_len, outer_len):
    full_len = inner_len * outer_len
    cos_turn, sin_turn = phase_table(inner_len, outer_len, full_len)
    first_re = first[..., :outer_len]
    first_im = first[..., outer_len:]
    turned = jnp.stack(
        [first_re * cos_turn + first_im * sin_turn, first_im * cos_turn - first_re * sin_turn],
        axis=-3,
    )
    cos_last, sin_last = phase_table(inner_len, inner_len, inner_len)
    return jnp.einsum(
        "...cnk,cne->...ke", turned, block_table(cos_last, sin_last), precision=TABLE_PRECISION
    )


def forward_pairs(values):
    inner_len = values.shape[-1]
    half_rows = values.shape[-2]
    outer_len = 2 * half_rows
    cos_first, sin_first = phase_table(half_rows, outer_len, outer_len)
    first = jnp.einsum(
        "fagmn,ame->fgne", values, block_table(cos_first, sin_first), precision=TABLE_PRECISION
    )
    return finish_forward(first, inner_len, outer_len)


def forward_real(values):
    inner_len = values.shape[-1]
    half_rows = values.shape[-2]
    outer_len = 2 * half_rows
    cos_first, sin_first = phase_table(half_rows, outer_len, outer_len)
    first = jnp.einsum(
        "fmn,me->fne", values, block_table(cos_first, sin_first)[0], precision=TABLE_PRECISION
    )
    return finish_forward(first, inner_len, outer_len)


def inverse_spectrum(spectrum, real_only):
    outer_len = spectrum.shape[-2]
    inner_len = spectrum.shape[-1] // 2
    half_rows = outer_len // 2
    full_len = outer_len * inner_len
    cos_first, sin_first = phase_table(inner_len, inner_len, inner_len)
    table_first = jnp.concatenate(
        [
            jnp.concatenate([cos_first, sin_first], axis=1),
            jnp.concatenate([-sin_first, cos_first], axis=1),
        ],
        axis=0,
    )
    step = jnp.einsum("...ke,ew->...kw", spectrum, table_first, precision=TABLE_PRECISION)
    step_re = step[..., :inner_len]
    step_im = step[..., inner_len:]
    cos_turn, sin_turn = phase_table(outer_len, inner_len, full_len)
    turned = jnp.stack(
        [step_re * cos_turn - step_im * sin_turn, step_re * sin_turn + step_im * cos_turn], axis=-3
    )
    cos_last, sin_last = phase_table(half_rows, outer_len, outer_len)
    table_last = jnp.stack(
        [jnp.stack([cos_last, -sin_last], axis=1), jnp.stack([sin_last, cos_last], axis=1)]
    )
    norm_factor = 1.0 / full_len
    if real_only:
        return (
            jnp.einsum("mck,...ckn->m...n", table_last[0], turned, precision=TABLE_PRECISION)
            * norm_factor
        )
    return (
        jnp.einsum("dmck,...ckn->dm...n", table_last, turned, precision=TABLE_PRECISION)
        * norm_factor
    )


def body(arriving, features, short_taps, filters):
    ctx_count = lax.axis_size("ctx")
    ctx_rank = lax.axis_index("ctx")
    dp_count = lax.axis_size("dp")
    rows_dev = features.shape[2]
    channels = features.shape[3]
    own_width = channels // ctx_count
    filter_count = filters.shape[1]
    group_size = own_width // filter_count
    half_group = group_size // 2
    taps_count = short_taps.shape[1]
    seq_len = filters.shape[2]
    inner_len = split_length(seq_len)
    half_rows = seq_len // inner_len
    feature_cols = features[0, 0].T
    arrived = passed_along(arriving, "pipe", -1)
    gradient_cols = arrived[0, 0].T
    gradient_block, feature_block = (
        lax.all_to_all(gradient_cols, "ctx", split_axis=0, concat_axis=1, tiled=True),
        lax.all_to_all(feature_cols, "ctx", split_axis=0, concat_axis=1, tiled=True),
    )
    tap_block = lax.dynamic_slice_in_dim(short_taps[0], ctx_rank * own_width, own_width, 1)
    feature_vals = feature_block.astype(jnp.float32)
    padded_feat = jnp.pad(feature_vals, ((0, 0), (taps_count - 1, 0)))
    conv_in = jnp.zeros(feature_vals.shape, jnp.float32)
    for offset in range(taps_count):
        conv_in = (
            conv_in
            + tap_block[offset][:, None]
            * padded_feat[:, taps_count - 1 - offset : taps_count - 1 - offset + seq_len]
        )
    pair_shape = (filter_count, 2, half_group, half_rows, inner_len)
    spectrum_u = forward_pairs(conv_in.reshape(pair_shape))
    spectrum_g = forward_pairs(gradient_block.astype(jnp.float32).reshape(pair_shape))
    spectrum_h = forward_real(filters[0].reshape(filter_count, half_rows, inner_len))[:, None]
    g_re = spectrum_g[..., :inner_len]
    g_im = spectrum_g[..., inner_len:]
    u_re = spectrum_u[..., :inner_len]
    u_im = spectrum_u[..., inner_len:]
    h_re = spectrum_h[..., :inner_len]
    h_im = spectrum_h[..., inner_len:]
    back = jnp.concatenate([h_re * g_re + h_im * g_im, h_re * g_im - h_im * g_re], axis=-1)
    lag = jnp.concatenate(
        [jnp.sum(g_re * u_re + g_im * u_im, axis=1), jnp.sum(g_im * u_re - g_re * u_im, axis=1)],
        axis=-1,
    )
    grad_blocks = inverse_spectrum(back, False)
    conv_in_grad = jnp.transpose(grad_blocks, (2, 0, 3, 1, 4)).reshape(own_width, seq_len)
    filter_part = jnp.transpose(inverse_spectrum(lag, True), (1, 0, 2)).reshape(
        filter_count, seq_len
    )
    padded_grad = jnp.pad(conv_in_grad, ((0, 0), (0, taps_count - 1)))
    feature_grad = jnp.zeros(conv_in_grad.shape, jnp.float32)
    tap_terms = []
    for offset in range(taps_count):
        feature_grad = (
            feature_grad + tap_block[offset][:, None] * padded_grad[:, offset : offset + seq_len]
        )
        tap_terms.append(
            jnp.sum(
                conv_in_grad
                * padded_feat[:, taps_count - 1 - offset : taps_count - 1 - offset + seq_len],
                axis=1,
            )
        )
    tap_part = jnp.stack(tap_terms)
    filter_total, tap_total = lax.psum((filter_part, tap_part), "dp")
    back_cols = feature_grad.astype(jnp.bfloat16)
    feature_rows = lax.all_to_all(back_cols, "ctx", split_axis=1, concat_axis=0, tiled=True)
    feature_grads = feature_rows.T.reshape(1, 1, rows_dev, channels)
    filter_scale = 1.0 / math.sqrt(dp_count * group_size * seq_len)
    tap_scale = 1.0 / math.sqrt(dp_count * seq_len)
    filter_grads = (filter_total * filter_scale)[None]
    tap_grads = (tap_total * tap_scale).reshape(1, taps_count, own_width)
    return (feature_grads, filter_grads, tap_grads)


def fused_kernel(
    sizes,
    arriving,
    features,
    taps_all,
    filters_all,
    feature_out,
    filter_out,
    tap_out,
    taps,
    filters,
    lent_filters,
    inbox,
    late_inbox,
    late_edge,
    outbox,
    late_outbox,
    shares,
    late_share,
    late_landed,
    wide_feat,
    split_in,
    grad_cols,
    turned,
    conv_cols,
    conv_grad,
    diagonals,
    local_sems,
    send_in,
    recv_in,
    recv_late,
    send_edge,
    recv_edge,
    send_lent,
    recv_lent,
    send_late,
    recv_landed,
    send_out,
    recv_out,
    send_share,
    recv_share,
):
    blocks, dp_count, pipe_count, chunks, rows, width, group, taps_count = sizes
    seq_len = blocks * rows
    half = blocks // 2
    own_width = chunks * width
    per_chunk = width // group
    me = lax.axis_index("ctx")
    dp_rank = lax.axis_index("dp")
    pipe_rank = lax.axis_index("pipe")
    before = lax.rem(pipe_rank + pipe_count - 1, pipe_count)
    is_early = me < half
    is_late = me >= half

    fetch_taps = pltpu.make_async_copy(taps_all, taps, local_sems.at[0])
    fetch_taps.start()
    fetch_filters = pltpu.make_async_copy(filters_all.at[0], filters, local_sems.at[1])
    fetch_filters.start()

    barrier = pltpu.get_barrier_semaphore()
    for step in range(1, blocks):
        pl.semaphore_signal(
            barrier,
            inc=1,
            device_id={"ctx": lax.rem(me + step, blocks)},
            device_id_type=MESH,
        )
    for step in range(blocks):
        pl.semaphore_signal(
            barrier,
            inc=1,
            device_id={"pipe": before, "ctx": lax.rem(me + step, blocks)},
            device_id_type=MESH,
        )
    for step in range(1, dp_count):
        pl.semaphore_signal(
            barrier,
            inc=1,
            device_id={"dp": lax.rem(dp_rank + step, dp_count)},
            device_id_type=MESH,
        )
    pl.semaphore_wait(barrier, 2 * blocks + dp_count - 2)

    def columns(owner, chunk):
        return pl.ds(pl.multiple_of(owner * own_width + chunk * width, width), width)

    def tap_rows_of(owner, chunk):
        place = owner * chunks + chunk
        return [taps[tap, pl.ds(place, 1), :] for tap in range(taps_count)]

    def send(source, target, send_sem, recv_sem, device):
        pltpu.make_async_remote_copy(
            src_ref=source,
            dst_ref=target,
            send_sem=send_sem,
            recv_sem=recv_sem,
            device_id=device,
            device_id_type=MESH,
        ).start()

    def send_chunk(chunk, carry):
        @pl.when(is_early)
        def _():
            send(
                filters_all.at[0, pl.ds(pl.multiple_of(chunk * per_chunk, 8), per_chunk), 0 : half * rows],
                lent_filters.at[chunk],
                send_lent,
                recv_lent.at[chunk],
                {"ctx": me + half},
            )

        @pl.when(me == half - 1)
        def _():
            for owner in range(half):
                send(
                    features.at[rows - 16 : rows, columns(owner, chunk)],
                    late_edge.at[chunk],
                    send_edge,
                    recv_edge.at[chunk],
                    {"ctx": half + owner},
                )

        @pl.when(is_late)
        def _():
            for step in range(half):
                owner = lax.rem(me + step, half)
                device = owner + half
                send(
                    arriving.at[:, columns(owner, chunk)],
                    late_inbox.at[chunk, me - half],
                    send_in,
                    recv_late.at[chunk],
                    {"pipe": before, "ctx": device},
                )
                if step:
                    send(
                        features.at[:, columns(owner, chunk)],
                        late_inbox.at[chunk, me],
                        send_in,
                        recv_late.at[chunk],
                        {"ctx": device},
                    )
                else:
                    pltpu.make_async_copy(
                        features.at[:, columns(owner, chunk)],
                        late_inbox.at[chunk, me],
                        recv_late.at[chunk],
                    ).start()

        for step in range(blocks):
            target = lax.rem(me + step, blocks)
            send(
                arriving.at[:, columns(target, chunk)],
                inbox.at[chunk, me],
                send_in,
                recv_in.at[chunk],
                {"pipe": before, "ctx": target},
            )
            if step:

                @pl.when(jnp.logical_or(is_early, target >= half))
                def _():
                    send(
                        features.at[:, columns(target, chunk)],
                        inbox.at[chunk, blocks + me],
                        send_in,
                        recv_in.at[chunk],
                        {"ctx": target},
                    )

        pltpu.make_async_copy(
            features.at[:, columns(me, chunk)], inbox.at[chunk, blocks + me], recv_in.at[chunk]
        ).start()
        return carry

    lax.fori_loop(0, chunks, send_chunk, 0)
    fetch_taps.wait()
    fetch_filters.wait()

    row_index = lax.broadcasted_iota(jnp.int32, (rows, rows), 0)
    lane_index = lax.broadcasted_iota(jnp.int32, (rows, rows), 1)
    upper = lane_index >= row_index
    lower = row_index >= lane_index
    mirror = (lax.rem(row_index + lane_index, rows) == 0).astype(jnp.bfloat16)
    zero_tile = jnp.zeros((rows, rows), jnp.float32)
    edge_zero = jnp.zeros((8, width), jnp.float32)
    zero_strip = jnp.zeros((16, rows), jnp.bfloat16)

    def convolve(tap_rows, feat_at, grad_at, kernel_rows, feat_blocks, grad_blocks):
        for block in range(feat_blocks):
            wide_feat[8 + block * rows : 8 + (block + 1) * rows, :] = feat_at(block).astype(
                jnp.float32
            )
        for block in range(feat_blocks):
            here = slice(block * rows, (block + 1) * rows)
            summed = zero_tile
            for tap in range(taps_count):
                start = 8 + block * rows - tap
                summed = summed + tap_rows[tap] * wide_feat[start : start + rows, :]
            summed = summed.T
            high = summed.astype(jnp.bfloat16)
            split_in[0, :, here] = high
            split_in[1, :, here] = (summed - high.astype(jnp.float32)).astype(jnp.bfloat16)
        for block in range(grad_blocks):
            grad_cols[:, block * rows : (block + 1) * rows] = grad_at(block).T
        grad_cols[:, grad_blocks * rows : (grad_blocks + feat_blocks - 1) * rows] = jnp.zeros(
            (width, (feat_blocks - 1) * rows), jnp.bfloat16
        )
        for block in range(grad_blocks):
            here = slice(block * rows, (block + 1) * rows)
            whole = kernel_rows[:, here]
            high = whole.astype(jnp.bfloat16)
            low = (whole - high.astype(jnp.float32)).astype(jnp.bfloat16)
            turned[:, here] = jnp.dot(
                high, mirror, preferred_element_type=jnp.float32
            ) + jnp.dot(low, mirror, preferred_element_type=jnp.float32)

        def one_filter(index):
            ours = pl.ds(pl.multiple_of(index * group, group), group)
            kernel_row = turned[pl.ds(index, 1), :]
            highs, lows = [], []
            last = [(zero_strip, zero_strip)] * (rows // 16)
            for block in range(grad_blocks):
                spread = jnp.broadcast_to(
                    kernel_row[:, block * rows : (block + 1) * rows], (16, rows)
                )
                base = pltpu.roll(spread, 0, 1, stride=1, stride_axis=0)
                high = base.astype(jnp.bfloat16)
                low = (base - high.astype(jnp.float32)).astype(jnp.bfloat16)
                strips = [
                    (
                        pltpu.roll(high, part * 16, 1) if part else high,
                        pltpu.roll(low, part * 16, 1) if part else low,
                    )
                    for part in range(rows // 16)
                ]
                for part in range(rows // 16):
                    keep = lower[part * 16 : part * 16 + 16]
                    highs.append(jnp.where(keep, strips[part][0], last[part][0]))
                    lows.append(jnp.where(keep, strips[part][1], last[part][1]))
                last = strips
            table = jnp.concatenate(
                [jnp.concatenate(highs, axis=0), jnp.concatenate(lows, axis=0)], axis=1
            )
            shifted = jnp.concatenate(
                [
                    grad_cols[ours, block * rows : (block + grad_blocks) * rows]
                    for block in range(feat_blocks)
                ],
                axis=0,
            )
            product = jnp.dot(shifted, table, preferred_element_type=jnp.float32)
            both = product[:, :rows] + product[:, rows:]
            for block in range(feat_blocks):
                conv_cols[ours, block * rows : (block + 1) * rows] = both[
                    block * group : (block + 1) * group
                ]
            picked = jnp.concatenate(
                [
                    split_in[part, ours, block * rows : (block + 1) * rows]
                    for part in range(2)
                    for block in range(feat_blocks)
                ],
                axis=0,
            )
            sums = jnp.dot(
                picked.T,
                jnp.concatenate([shifted, shifted], axis=0),
                preferred_element_type=jnp.float32,
            )
            for lag in range(grad_blocks):
                following = (
                    sums[:, (lag + 1) * rows : (lag + 2) * rows]
                    if lag + 1 < grad_blocks
                    else zero_tile
                )
                merged = jnp.where(upper, sums[:, lag * rows : (lag + 1) * rows], following)
                folded = [merged[0:8]]
                for part in range(1, rows // 8):
                    folded.append(
                        pltpu.roll(merged[part * 8 : part * 8 + 8], rows - part * 8, 1)
                    )
                while len(folded) > 1:
                    folded = [
                        folded[place] + folded[place + 1] for place in range(0, len(folded), 2)
                    ]
                place = pl.multiple_of((lag * per_chunk + index) * 8, 8)
                diagonals[pl.ds(place, 8), :] = folded[0]

        def do_filters(index, inner):
            one_filter(2 * index)
            one_filter(2 * index + 1)
            return inner

        lax.fori_loop(0, per_chunk // 2, do_filters, 0)
        for block in range(feat_blocks):
            here = slice(block * rows, (block + 1) * rows)
            conv_grad[here, :] = conv_cols[:, here].T
        count = grad_blocks * per_chunk
        lagged = diagonals[pl.ds(0, count, stride=8), :]
        for turn in range(1, 8):
            lagged = lagged + pltpu.roll(
                diagonals[pl.ds(turn, count, stride=8), :], rows - turn, 1
            )
        return [
            lagged[lag * per_chunk : (lag + 1) * per_chunk] for lag in range(grad_blocks)
        ]

    def finish(tap_rows, feat_blocks, put):
        tap_sums = [edge_zero] * taps_count
        for block in range(feat_blocks):
            here = block * rows
            summed = zero_tile
            feats = wide_feat[8 + here : 8 + here + rows, :]
            for tap in range(taps_count):
                grads = conv_grad[here + tap : here + tap + rows, :]
                summed = summed + tap_rows[tap] * grads
                pairs = grads * feats
                tap_sums[tap] = tap_sums[tap] + jnp.sum(
                    pairs.reshape(rows // 8, 8, width), axis=0
                )
            put(block, summed.astype(jnp.bfloat16))
        tap_sums = [jnp.sum(value, axis=0, keepdims=True) for value in tap_sums]
        if per_chunk > taps_count:
            tap_sums.append(jnp.zeros((per_chunk - taps_count, width), jnp.float32))
        return jnp.concatenate(tap_sums, axis=0)


    def put_out(chunk):
        def put(block, value):
            outbox[chunk, block] = value

        return put

    def keep_shares(chunk, lags, tap_share):
        for lag in range(blocks):
            shares[dp_rank, chunk, :, lag * rows : (lag + 1) * rows] = lags[lag]
        shares[dp_rank, chunk, :, seq_len : seq_len + width] = tap_share

    def send_shares(chunk):
        for step in range(1, dp_count):
            send(
                shares.at[dp_rank, chunk],
                shares.at[dp_rank, chunk],
                send_share,
                recv_share,
                {"dp": lax.rem(dp_rank + step, dp_count)},
            )

    def own_columns(chunk):
        return feature_out.at[:, columns(me, chunk)]

    def do_early(chunk, carry):
        landed = inbox.at[chunk, 0 : blocks + half]
        pltpu.make_async_copy(landed, landed, recv_in.at[chunk]).wait()
        tap_rows = tap_rows_of(me, chunk)
        wide_feat[0:8, :] = edge_zero
        lags = convolve(
            tap_rows,
            lambda block: inbox[chunk, blocks + block],
            lambda block: inbox[chunk, block],
            filters[pl.ds(pl.multiple_of(chunk * per_chunk, 8), per_chunk), :],
            half,
            blocks,
        )
        bundle = late_landed.at[chunk]
        pltpu.make_async_copy(bundle, bundle, recv_landed.at[chunk]).wait()
        lent = half * rows
        conv_grad[lent : lent + 8, :] = late_landed[chunk, :, lent + width : lent + 2 * width]
        tap_share = finish(tap_rows, half, put_out(chunk))
        tap_share = tap_share + late_landed[chunk, :, lent : lent + width]
        for lag in range(half):
            lags[lag] = lags[lag] + late_landed[chunk, :, lag * rows : (lag + 1) * rows]
        keep_shares(chunk, lags, tap_share)
        other = half - 1 - me
        send(outbox.at[chunk, other], own_columns(chunk), send_out, recv_out, {"ctx": other})
        pltpu.make_async_copy(outbox.at[chunk, me], own_columns(chunk), recv_out).start()
        send_shares(chunk)
        return carry

    def do_late(chunk, carry):
        owner = me - half
        landed = late_inbox.at[chunk]
        pltpu.make_async_copy(landed, landed, recv_late.at[chunk]).wait()
        edge = late_edge.at[chunk]
        pltpu.make_async_copy(edge, edge, recv_edge.at[chunk]).wait()
        lent_here = lent_filters.at[chunk]
        pltpu.make_async_copy(lent_here, lent_here, recv_lent.at[chunk]).wait()
        tap_rows = tap_rows_of(owner, chunk)
        wide_feat[0:8, :] = late_edge[chunk].astype(jnp.float32)[8:16]
        lags = convolve(
            tap_rows,
            lambda block: late_inbox[chunk, half + block],
            lambda block: late_inbox[chunk, block],
            lent_filters[chunk],
            half,
            half,
        )
        conv_grad[half * rows : half * rows + 8, :] = edge_zero

        def put(block, value):
            late_outbox[chunk, block] = value

        tap_share = finish(tap_rows, half, put)
        lent = half * rows
        for lag in range(half):
            late_share[chunk, :, lag * rows : (lag + 1) * rows] = lags[lag]
        late_share[chunk, :, lent : lent + width] = tap_share
        late_share[chunk, :, lent + width : lent + 2 * width] = conv_grad[0:8, :]
        send(
            late_share.at[chunk],
            late_landed.at[chunk],
            send_late,
            recv_landed.at[chunk],
            {"ctx": owner},
        )
        place = feature_out.at[:, columns(owner, chunk)]
        other = half - 1 - owner
        send(late_outbox.at[chunk, other], place, send_out, recv_out, {"ctx": half + other})
        pltpu.make_async_copy(late_outbox.at[chunk, owner], place, recv_out).start()

        landed = inbox.at[chunk]
        pltpu.make_async_copy(landed, landed, recv_in.at[chunk]).wait()
        tap_rows = tap_rows_of(me, chunk)
        wide_feat[0:8, :] = edge_zero
        lags = convolve(
            tap_rows,
            lambda block: inbox[chunk, blocks + block],
            lambda block: inbox[chunk, block],
            filters[pl.ds(pl.multiple_of(chunk * per_chunk, 8), per_chunk), :],
            blocks,
            blocks,
        )
        conv_grad[seq_len : seq_len + 8, :] = edge_zero
        tap_share = finish(tap_rows, blocks, put_out(chunk))
        keep_shares(chunk, lags, tap_share)
        for step in range(1, blocks):
            target = lax.rem(me + step, blocks)
            send(
                outbox.at[chunk, target], own_columns(chunk), send_out, recv_out, {"ctx": target}
            )
        pltpu.make_async_copy(outbox.at[chunk, me], own_columns(chunk), recv_out).start()
        send_shares(chunk)
        return carry

    def drain(ref, sem):
        pltpu.make_async_copy(ref, ref, sem).wait()

    @pl.when(is_early)
    def _():
        lax.fori_loop(0, chunks, do_early, 0)

    @pl.when(is_late)
    def _():
        lax.fori_loop(0, chunks, do_late, 0)

    drain(shares.at[0 : dp_count - 1], recv_share)
    filter_scale = 1.0 / math.sqrt(dp_count * group * seq_len)
    tap_scale = 1.0 / math.sqrt(dp_count * seq_len)
    for chunk in range(chunks):
        total = shares[0, chunk]
        for rank in range(1, dp_count):
            total = total + shares[rank, chunk]
        filter_out[chunk * per_chunk : (chunk + 1) * per_chunk, :] = (
            total[:, :seq_len] * filter_scale
        )
        tap_out[:, chunk * width : (chunk + 1) * width] = total[:taps_count, seq_len:] * tap_scale
    drain(shares.at[0 : dp_count - 1], send_share)

    @pl.when(is_early)
    def _():
        drain(lent_filters, send_lent)
        drain(inbox.at[:, 0 : 2 * blocks - 1], send_in)
        drain(outbox.at[:, 0 : half - 1], send_out)

    @pl.when(me == half - 1)
    def _():
        for _ in range(half):
            drain(late_edge, send_edge)

    @pl.when(is_late)
    def _():
        drain(inbox, send_in)
        drain(outbox, send_out)
        drain(late_share, send_late)

    drain(outbox, recv_out)


def fused_body(arriving, features, short_taps, filters):
    blocks = lax.axis_size("ctx")
    dp_count = lax.axis_size("dp")
    pipe_count = lax.axis_size("pipe")
    rows, channels = features.shape[2], features.shape[3]
    own_width = channels // blocks
    filter_count, seq_len = filters.shape[1], filters.shape[2]
    group = own_width // filter_count
    taps_count = short_taps.shape[1]
    width = rows
    half = blocks // 2
    chunks = own_width // width
    per_chunk = width // group
    lent = half * rows
    sizes = (blocks, dp_count, pipe_count, chunks, rows, width, group, taps_count)
    anywhere = pl.BlockSpec(memory_space=pltpu.HBM)
    vmem = pl.BlockSpec(memory_space=pltpu.VMEM)
    one_sem = pltpu.SemaphoreType.DMA
    chunk_sems = pltpu.SemaphoreType.DMA((chunks,))
    feature_grads, filter_grads, tap_grads = pl.pallas_call(
        functools.partial(fused_kernel, sizes),
        out_shape=(
            jax.ShapeDtypeStruct((rows, channels), jnp.bfloat16),
            jax.ShapeDtypeStruct((filter_count, seq_len), jnp.float32),
            jax.ShapeDtypeStruct((taps_count, own_width), jnp.float32),
        ),
        in_specs=[anywhere] * 4,
        out_specs=(anywhere, vmem, vmem),
        scratch_shapes=[
            pltpu.VMEM((taps_count, channels // width, width), jnp.float32),
            pltpu.VMEM((filter_count, seq_len), jnp.float32),
            pltpu.VMEM((chunks, per_chunk, lent), jnp.float32),
            pltpu.VMEM((chunks, 2 * blocks, rows, width), jnp.bfloat16),
            pltpu.VMEM((chunks, 2 * half, rows, width), jnp.bfloat16),
            pltpu.VMEM((chunks, 16, width), jnp.bfloat16),
            pltpu.VMEM((chunks, blocks, rows, width), jnp.bfloat16),
            pltpu.VMEM((chunks, half, rows, width), jnp.bfloat16),
            pltpu.VMEM((dp_count, chunks, per_chunk, seq_len + width), jnp.float32),
            pltpu.VMEM((chunks, per_chunk, lent + 2 * width), jnp.float32),
            pltpu.VMEM((chunks, per_chunk, lent + 2 * width), jnp.float32),
            pltpu.VMEM((seq_len + 8, width), jnp.float32),
            pltpu.VMEM((2, width, seq_len), jnp.bfloat16),
            pltpu.VMEM((width, 2 * seq_len), jnp.bfloat16),
            pltpu.VMEM((per_chunk, seq_len), jnp.float32),
            pltpu.VMEM((width, seq_len), jnp.float32),
            pltpu.VMEM((seq_len + 8, width), jnp.float32),
            pltpu.VMEM((blocks * per_chunk * 8, width), jnp.float32),
            pltpu.SemaphoreType.DMA((2,)),
            one_sem,
            chunk_sems,
            chunk_sems,
            one_sem,
            chunk_sems,
            one_sem,
            chunk_sems,
            one_sem,
            chunk_sems,
            one_sem,
            one_sem,
            one_sem,
            one_sem,
        ],
        compiler_params=pltpu.CompilerParams(
            collective_id=0, has_side_effects=True, vmem_limit_bytes=60 * 1024 * 1024
        ),
    )(
        arriving[0, 0],
        features[0, 0],
        short_taps.reshape(taps_count, channels // width, width),
        filters,
    )
    return (feature_grads[None, None], filter_grads[None], tap_grads[None])


def fits_fused(mesh, features, short_taps, filters):
    blocks, rows = mesh.shape["ctx"], features.shape[2] // mesh.shape["ctx"]
    own_width = features.shape[3] // blocks
    own_filters = filters.shape[1] // blocks
    group = own_width // own_filters
    return (
        rows == 128
        and blocks == 4
        and mesh.shape["pipe"] == 2
        and own_width % rows == 0
        and rows % group == 0
        and rows // group == 8
        and short_taps.shape[1] <= 8
    )


def solution(mesh):
    in_specs = (
        P("pipe", "dp", "ctx", None),
        P("pipe", "dp", "ctx", None),
        P("pipe", None, None),
        P("pipe", "ctx", None),
    )
    out_specs = (P("pipe", "dp", "ctx", None), P("pipe", "ctx", None), P("pipe", None, "ctx"))

    def run(arriving, features, short_taps, filters):
        chosen = fused_body if fits_fused(mesh, features, short_taps, filters) else body
        return jax.shard_map(
            chosen, mesh=mesh, in_specs=in_specs, out_specs=out_specs, check_vma=False
        )(arriving, features, short_taps, filters)

    return run
```

```python
import functools
import math

import jax
import jax.numpy as jnp
from jax import lax
from jax.experimental import pallas as pl
from jax.experimental.pallas import tpu as pltpu
from jax.sharding import PartitionSpec as P

TABLE_PRECISION = lax.Precision.HIGH
MESH = pl.DeviceIdType.MESH


def passed_along(value, axis, steps):
    count = lax.axis_size(axis)
    pairs = [(source, (source + steps) % count) for source in range(count)]
    return lax.ppermute(value, axis, pairs)


def phase_table(count_a, count_b, modulus):
    first_index = lax.broadcasted_iota(jnp.int32, (count_a, count_b), 0)
    second_index = lax.broadcasted_iota(jnp.int32, (count_a, count_b), 1)
    phase = (first_index * second_index % modulus).astype(jnp.float32) * (2.0 * math.pi / modulus)
    return (jnp.cos(phase), jnp.sin(phase))


def block_table(cos_part, sin_part):
    return jnp.stack(
        [
            jnp.concatenate([cos_part, -sin_part], axis=-1),
            jnp.concatenate([sin_part, cos_part], axis=-1),
        ]
    )


def split_length(seq_len):
    factor = 1
    for candidate in range(1, seq_len + 1):
        if seq_len % candidate == 0 and candidate * candidate <= 2 * seq_len:
            factor = candidate
    return factor


def finish_forward(first, inner_len, outer_len):
    full_len = inner_len * outer_len
    cos_turn, sin_turn = phase_table(inner_len, outer_len, full_len)
    first_re = first[..., :outer_len]
    first_im = first[..., outer_len:]
    turned = jnp.stack(
        [first_re * cos_turn + first_im * sin_turn, first_im * cos_turn - first_re * sin_turn],
        axis=-3,
    )
    cos_last, sin_last = phase_table(inner_len, inner_len, inner_len)
    return jnp.einsum(
        "...cnk,cne->...ke", turned, block_table(cos_last, sin_last), precision=TABLE_PRECISION
    )


def forward_pairs(values):
    inner_len = values.shape[-1]
    half_rows = values.shape[-2]
    outer_len = 2 * half_rows
    cos_first, sin_first = phase_table(half_rows, outer_len, outer_len)
    first = jnp.einsum(
        "fagmn,ame->fgne", values, block_table(cos_first, sin_first), precision=TABLE_PRECISION
    )
    return finish_forward(first, inner_len, outer_len)


def forward_real(values):
    inner_len = values.shape[-1]
    half_rows = values.shape[-2]
    outer_len = 2 * half_rows
    cos_first, sin_first = phase_table(half_rows, outer_len, outer_len)
    first = jnp.einsum(
        "fmn,me->fne", values, block_table(cos_first, sin_first)[0], precision=TABLE_PRECISION
    )
    return finish_forward(first, inner_len, outer_len)


def inverse_spectrum(spectrum, real_only):
    outer_len = spectrum.shape[-2]
    inner_len = spectrum.shape[-1] // 2
    half_rows = outer_len // 2
    full_len = outer_len * inner_len
    cos_first, sin_first = phase_table(inner_len, inner_len, inner_len)
    table_first = jnp.concatenate(
        [
            jnp.concatenate([cos_first, sin_first], axis=1),
            jnp.concatenate([-sin_first, cos_first], axis=1),
        ],
        axis=0,
    )
    step = jnp.einsum("...ke,ew->...kw", spectrum, table_first, precision=TABLE_PRECISION)
    step_re = step[..., :inner_len]
    step_im = step[..., inner_len:]
    cos_turn, sin_turn = phase_table(outer_len, inner_len, full_len)
    turned = jnp.stack(
        [step_re * cos_turn - step_im * sin_turn, step_re * sin_turn + step_im * cos_turn], axis=-3
    )
    cos_last, sin_last = phase_table(half_rows, outer_len, outer_len)
    table_last = jnp.stack(
        [jnp.stack([cos_last, -sin_last], axis=1), jnp.stack([sin_last, cos_last], axis=1)]
    )
    norm_factor = 1.0 / full_len
    if real_only:
        return (
            jnp.einsum("mck,...ckn->m...n", table_last[0], turned, precision=TABLE_PRECISION)
            * norm_factor
        )
    return (
        jnp.einsum("dmck,...ckn->dm...n", table_last, turned, precision=TABLE_PRECISION)
        * norm_factor
    )


def body(arriving, features, short_taps, filters):
    ctx_count = lax.axis_size("ctx")
    ctx_rank = lax.axis_index("ctx")
    dp_count = lax.axis_size("dp")
    rows_dev = features.shape[2]
    channels = features.shape[3]
    own_width = channels // ctx_count
    filter_count = filters.shape[1]
    group_size = own_width // filter_count
    half_group = group_size // 2
    taps_count = short_taps.shape[1]
    seq_len = filters.shape[2]
    inner_len = split_length(seq_len)
    half_rows = seq_len // inner_len
    feature_cols = features[0, 0].T
    arrived = passed_along(arriving, "pipe", -1)
    gradient_cols = arrived[0, 0].T
    gradient_block, feature_block = (
        lax.all_to_all(gradient_cols, "ctx", split_axis=0, concat_axis=1, tiled=True),
        lax.all_to_all(feature_cols, "ctx", split_axis=0, concat_axis=1, tiled=True),
    )
    tap_block = lax.dynamic_slice_in_dim(short_taps[0], ctx_rank * own_width, own_width, 1)
    feature_vals = feature_block.astype(jnp.float32)
    padded_feat = jnp.pad(feature_vals, ((0, 0), (taps_count - 1, 0)))
    conv_in = jnp.zeros(feature_vals.shape, jnp.float32)
    for offset in range(taps_count):
        conv_in = (
            conv_in
            + tap_block[offset][:, None]
            * padded_feat[:, taps_count - 1 - offset : taps_count - 1 - offset + seq_len]
        )
    pair_shape = (filter_count, 2, half_group, half_rows, inner_len)
    spectrum_u = forward_pairs(conv_in.reshape(pair_shape))
    spectrum_g = forward_pairs(gradient_block.astype(jnp.float32).reshape(pair_shape))
    spectrum_h = forward_real(filters[0].reshape(filter_count, half_rows, inner_len))[:, None]
    g_re = spectrum_g[..., :inner_len]
    g_im = spectrum_g[..., inner_len:]
    u_re = spectrum_u[..., :inner_len]
    u_im = spectrum_u[..., inner_len:]
    h_re = spectrum_h[..., :inner_len]
    h_im = spectrum_h[..., inner_len:]
    back = jnp.concatenate([h_re * g_re + h_im * g_im, h_re * g_im - h_im * g_re], axis=-1)
    lag = jnp.concatenate(
        [jnp.sum(g_re * u_re + g_im * u_im, axis=1), jnp.sum(g_im * u_re - g_re * u_im, axis=1)],
        axis=-1,
    )
    grad_blocks = inverse_spectrum(back, False)
    conv_in_grad = jnp.transpose(grad_blocks, (2, 0, 3, 1, 4)).reshape(own_width, seq_len)
    filter_part = jnp.transpose(inverse_spectrum(lag, True), (1, 0, 2)).reshape(
        filter_count, seq_len
    )
    padded_grad = jnp.pad(conv_in_grad, ((0, 0), (0, taps_count - 1)))
    feature_grad = jnp.zeros(conv_in_grad.shape, jnp.float32)
    tap_terms = []
    for offset in range(taps_count):
        feature_grad = (
            feature_grad + tap_block[offset][:, None] * padded_grad[:, offset : offset + seq_len]
        )
        tap_terms.append(
            jnp.sum(
                conv_in_grad
                * padded_feat[:, taps_count - 1 - offset : taps_count - 1 - offset + seq_len],
                axis=1,
            )
        )
    tap_part = jnp.stack(tap_terms)
    filter_total, tap_total = lax.psum((filter_part, tap_part), "dp")
    back_cols = feature_grad.astype(jnp.bfloat16)
    feature_rows = lax.all_to_all(back_cols, "ctx", split_axis=1, concat_axis=0, tiled=True)
    feature_grads = feature_rows.T.reshape(1, 1, rows_dev, channels)
    filter_scale = 1.0 / math.sqrt(dp_count * group_size * seq_len)
    tap_scale = 1.0 / math.sqrt(dp_count * seq_len)
    filter_grads = (filter_total * filter_scale)[None]
    tap_grads = (tap_total * tap_scale).reshape(1, taps_count, own_width)
    return (feature_grads, filter_grads, tap_grads)


def fused_kernel(
    sizes,
    arriving,
    features,
    taps_all,
    filters_all,
    feature_out,
    filter_out,
    tap_out,
    taps,
    filters,
    lent_filters,
    inbox,
    late_inbox,
    late_edge,
    outbox,
    late_outbox,
    shares,
    late_share,
    late_landed,
    wide_feat,
    split_in,
    grad_cols,
    turned,
    conv_cols,
    conv_grad,
    diagonals,
    local_sems,
    send_in,
    recv_in,
    recv_late,
    send_edge,
    recv_edge,
    send_lent,
    recv_lent,
    send_late,
    recv_landed,
    send_out,
    recv_out,
    send_share,
    recv_share,
):
    blocks, dp_count, pipe_count, chunks, halved, rows, width, group, taps_count = sizes
    seq_len = blocks * rows
    half = blocks // 2
    own_width = chunks * width
    per_chunk = width // group
    me = lax.axis_index("ctx")
    dp_rank = lax.axis_index("dp")
    pipe_rank = lax.axis_index("pipe")
    before = lax.rem(pipe_rank + pipe_count - 1, pipe_count)
    is_early = me < half
    is_late = me >= half

    fetch_taps = pltpu.make_async_copy(taps_all, taps, local_sems.at[0])
    fetch_taps.start()
    fetch_filters = pltpu.make_async_copy(filters_all.at[0], filters, local_sems.at[1])
    fetch_filters.start()

    barrier = pltpu.get_barrier_semaphore()
    for step in range(1, blocks):
        pl.semaphore_signal(
            barrier,
            inc=1,
            device_id={"ctx": lax.rem(me + step, blocks)},
            device_id_type=MESH,
        )
    for step in range(blocks):
        pl.semaphore_signal(
            barrier,
            inc=1,
            device_id={"pipe": before, "ctx": lax.rem(me + step, blocks)},
            device_id_type=MESH,
        )
    for step in range(1, dp_count):
        pl.semaphore_signal(
            barrier,
            inc=1,
            device_id={"dp": lax.rem(dp_rank + step, dp_count)},
            device_id_type=MESH,
        )
    pl.semaphore_wait(barrier, 2 * blocks + dp_count - 2)

    def columns(owner, chunk):
        return pl.ds(pl.multiple_of(owner * own_width + chunk * width, width), width)

    def tap_rows_of(owner, chunk):
        place = owner * chunks + chunk
        return [taps[tap, pl.ds(place, 1), :] for tap in range(taps_count)]

    def send(source, target, send_sem, recv_sem, device):
        pltpu.make_async_remote_copy(
            src_ref=source,
            dst_ref=target,
            send_sem=send_sem,
            recv_sem=recv_sem,
            device_id=device,
            device_id_type=MESH,
        ).start()

    def send_chunk(chunk, carry):
        is_halved = chunk < halved

        @pl.when(jnp.logical_and(is_early, is_halved))
        def _():
            send(
                filters_all.at[0, pl.ds(pl.multiple_of(chunk * per_chunk, 8), per_chunk), 0 : half * rows],
                lent_filters.at[chunk],
                send_lent,
                recv_lent.at[chunk],
                {"ctx": me + half},
            )

        @pl.when(jnp.logical_and(me == half - 1, is_halved))
        def _():
            for owner in range(half):
                send(
                    features.at[rows - 16 : rows, columns(owner, chunk)],
                    late_edge.at[chunk],
                    send_edge,
                    recv_edge.at[chunk],
                    {"ctx": half + owner},
                )

        @pl.when(jnp.logical_and(is_late, is_halved))
        def _():
            for step in range(half):
                owner = lax.rem(me + step, half)
                device = owner + half
                send(
                    arriving.at[:, columns(owner, chunk)],
                    late_inbox.at[chunk, me - half],
                    send_in,
                    recv_late.at[chunk],
                    {"pipe": before, "ctx": device},
                )
                if step:
                    send(
                        features.at[:, columns(owner, chunk)],
                        late_inbox.at[chunk, me],
                        send_in,
                        recv_late.at[chunk],
                        {"ctx": device},
                    )
                else:
                    pltpu.make_async_copy(
                        features.at[:, columns(owner, chunk)],
                        late_inbox.at[chunk, me],
                        recv_late.at[chunk],
                    ).start()

        for step in range(blocks):
            target = lax.rem(me + step, blocks)
            send(
                arriving.at[:, columns(target, chunk)],
                inbox.at[chunk, me],
                send_in,
                recv_in.at[chunk],
                {"pipe": before, "ctx": target},
            )
            if step:

                @pl.when(
                    jnp.logical_or(
                        jnp.logical_or(is_early, target >= half), jnp.logical_not(is_halved)
                    )
                )
                def _():
                    send(
                        features.at[:, columns(target, chunk)],
                        inbox.at[chunk, blocks + me],
                        send_in,
                        recv_in.at[chunk],
                        {"ctx": target},
                    )

        pltpu.make_async_copy(
            features.at[:, columns(me, chunk)], inbox.at[chunk, blocks + me], recv_in.at[chunk]
        ).start()
        return carry

    lax.fori_loop(0, chunks, send_chunk, 0)
    fetch_taps.wait()
    fetch_filters.wait()

    row_index = lax.broadcasted_iota(jnp.int32, (rows, rows), 0)
    lane_index = lax.broadcasted_iota(jnp.int32, (rows, rows), 1)
    upper = lane_index >= row_index
    lower = row_index >= lane_index
    mirror = (lax.rem(row_index + lane_index, rows) == 0).astype(jnp.bfloat16)
    zero_tile = jnp.zeros((rows, rows), jnp.float32)
    edge_zero = jnp.zeros((8, width), jnp.float32)

    def convolve(tap_rows, feat_at, grad_at, kernel_rows, feat_blocks, grad_blocks):
        for block in range(feat_blocks):
            wide_feat[8 + block * rows : 8 + (block + 1) * rows, :] = feat_at(block).astype(
                jnp.float32
            )
        for block in range(feat_blocks):
            here = slice(block * rows, (block + 1) * rows)
            summed = zero_tile
            for tap in range(taps_count):
                start = 8 + block * rows - tap
                summed = summed + tap_rows[tap] * wide_feat[start : start + rows, :]
            summed = summed.T
            high = summed.astype(jnp.bfloat16)
            split_in[0, :, here] = high
            split_in[1, :, here] = (summed - high.astype(jnp.float32)).astype(jnp.bfloat16)
        for block in range(grad_blocks):
            grad_cols[:, block * rows : (block + 1) * rows] = grad_at(block).T
        grad_cols[:, grad_blocks * rows : (grad_blocks + feat_blocks - 1) * rows] = jnp.zeros(
            (width, (feat_blocks - 1) * rows), jnp.bfloat16
        )
        for block in range(grad_blocks):
            here = slice(block * rows, (block + 1) * rows)
            whole = kernel_rows[:, here]
            high = whole.astype(jnp.bfloat16)
            low = (whole - high.astype(jnp.float32)).astype(jnp.bfloat16)
            turned[:, here] = jnp.dot(
                high, mirror, preferred_element_type=jnp.float32
            ) + jnp.dot(low, mirror, preferred_element_type=jnp.float32)

        def one_filter(index):
            ours = pl.ds(pl.multiple_of(index * group, group), group)
            kernel_row = turned[pl.ds(index, 1), :]
            highs, lows = [], []
            last = zero_tile
            for block in range(grad_blocks):
                spread = jnp.broadcast_to(
                    kernel_row[:, block * rows : (block + 1) * rows], (rows, rows)
                )
                rolled = pltpu.roll(spread, 0, 1, stride=1, stride_axis=0)
                tile = jnp.where(lower, rolled, last)
                last = rolled
                high = tile.astype(jnp.bfloat16)
                highs.append(high)
                lows.append((tile - high.astype(jnp.float32)).astype(jnp.bfloat16))
            table = jnp.concatenate(
                [jnp.concatenate(highs, axis=0), jnp.concatenate(lows, axis=0)], axis=1
            )
            shifted = jnp.concatenate(
                [
                    grad_cols[ours, block * rows : (block + grad_blocks) * rows]
                    for block in range(feat_blocks)
                ],
                axis=0,
            )
            product = jnp.dot(shifted, table, preferred_element_type=jnp.float32)
            both = product[:, :rows] + product[:, rows:]
            for block in range(feat_blocks):
                conv_cols[ours, block * rows : (block + 1) * rows] = both[
                    block * group : (block + 1) * group
                ]
            picked = jnp.concatenate(
                [
                    split_in[part, ours, block * rows : (block + 1) * rows]
                    for part in range(2)
                    for block in range(feat_blocks)
                ],
                axis=0,
            )
            sums = jnp.dot(
                picked.T,
                jnp.concatenate([shifted, shifted], axis=0),
                preferred_element_type=jnp.float32,
            )
            for lag in range(grad_blocks):
                following = (
                    sums[:, (lag + 1) * rows : (lag + 2) * rows]
                    if lag + 1 < grad_blocks
                    else zero_tile
                )
                merged = jnp.where(upper, sums[:, lag * rows : (lag + 1) * rows], following)
                folded = [merged[0:8]]
                for part in range(1, rows // 8):
                    folded.append(
                        pltpu.roll(merged[part * 8 : part * 8 + 8], rows - part * 8, 1)
                    )
                while len(folded) > 1:
                    folded = [
                        folded[place] + folded[place + 1] for place in range(0, len(folded), 2)
                    ]
                place = pl.multiple_of((lag * per_chunk + index) * 8, 8)
                diagonals[pl.ds(place, 8), :] = folded[0]

        def do_filters(index, inner):
            one_filter(2 * index)
            one_filter(2 * index + 1)
            return inner

        lax.fori_loop(0, per_chunk // 2, do_filters, 0)
        for block in range(feat_blocks):
            here = slice(block * rows, (block + 1) * rows)
            conv_grad[here, :] = conv_cols[:, here].T
        count = grad_blocks * per_chunk
        lagged = diagonals[pl.ds(0, count, stride=8), :]
        for turn in range(1, 8):
            lagged = lagged + pltpu.roll(
                diagonals[pl.ds(turn, count, stride=8), :], rows - turn, 1
            )
        return [
            lagged[lag * per_chunk : (lag + 1) * per_chunk] for lag in range(grad_blocks)
        ]

    def finish(tap_rows, feat_blocks, put):
        tap_sums = [edge_zero] * taps_count
        for block in range(feat_blocks):
            here = block * rows
            summed = zero_tile
            feats = wide_feat[8 + here : 8 + here + rows, :]
            for tap in range(taps_count):
                grads = conv_grad[here + tap : here + tap + rows, :]
                summed = summed + tap_rows[tap] * grads
                pairs = grads * feats
                tap_sums[tap] = tap_sums[tap] + jnp.sum(
                    pairs.reshape(rows // 8, 8, width), axis=0
                )
            put(block, summed.astype(jnp.bfloat16))
        tap_sums = [jnp.sum(value, axis=0, keepdims=True) for value in tap_sums]
        if per_chunk > taps_count:
            tap_sums.append(jnp.zeros((per_chunk - taps_count, width), jnp.float32))
        return jnp.concatenate(tap_sums, axis=0)


    def put_out(chunk):
        def put(block, value):
            outbox[chunk, block] = value

        return put

    def keep_shares(chunk, lags, tap_share):
        for lag in range(blocks):
            shares[dp_rank, chunk, :, lag * rows : (lag + 1) * rows] = lags[lag]
        shares[dp_rank, chunk, :, seq_len : seq_len + width] = tap_share

    def send_shares(chunk):
        for step in range(1, dp_count):
            send(
                shares.at[dp_rank, chunk],
                shares.at[dp_rank, chunk],
                send_share,
                recv_share,
                {"dp": lax.rem(dp_rank + step, dp_count)},
            )

    def own_columns(chunk):
        return feature_out.at[:, columns(me, chunk)]

    def do_early(chunk):
        landed = inbox.at[chunk, 0 : blocks + half]
        pltpu.make_async_copy(landed, landed, recv_in.at[chunk]).wait()
        tap_rows = tap_rows_of(me, chunk)
        wide_feat[0:8, :] = edge_zero
        lags = convolve(
            tap_rows,
            lambda block: inbox[chunk, blocks + block],
            lambda block: inbox[chunk, block],
            filters[pl.ds(pl.multiple_of(chunk * per_chunk, 8), per_chunk), :],
            half,
            blocks,
        )
        bundle = late_landed.at[chunk]
        pltpu.make_async_copy(bundle, bundle, recv_landed.at[chunk]).wait()
        lent = half * rows
        conv_grad[lent : lent + 8, :] = late_landed[chunk, :, lent + width : lent + 2 * width]
        tap_share = finish(tap_rows, half, put_out(chunk))
        tap_share = tap_share + late_landed[chunk, :, lent : lent + width]
        for lag in range(half):
            lags[lag] = lags[lag] + late_landed[chunk, :, lag * rows : (lag + 1) * rows]
        keep_shares(chunk, lags, tap_share)
        other = half - 1 - me
        send(outbox.at[chunk, other], own_columns(chunk), send_out, recv_out, {"ctx": other})
        pltpu.make_async_copy(outbox.at[chunk, me], own_columns(chunk), recv_out).start()
        send_shares(chunk)

    def do_late(chunk):
        owner = me - half
        landed = late_inbox.at[chunk]
        pltpu.make_async_copy(landed, landed, recv_late.at[chunk]).wait()
        edge = late_edge.at[chunk]
        pltpu.make_async_copy(edge, edge, recv_edge.at[chunk]).wait()
        lent_here = lent_filters.at[chunk]
        pltpu.make_async_copy(lent_here, lent_here, recv_lent.at[chunk]).wait()
        tap_rows = tap_rows_of(owner, chunk)
        wide_feat[0:8, :] = late_edge[chunk].astype(jnp.float32)[8:16]
        lags = convolve(
            tap_rows,
            lambda block: late_inbox[chunk, half + block],
            lambda block: late_inbox[chunk, block],
            lent_filters[chunk],
            half,
            half,
        )
        conv_grad[half * rows : half * rows + 8, :] = edge_zero

        def put(block, value):
            late_outbox[chunk, block] = value

        tap_share = finish(tap_rows, half, put)
        lent = half * rows
        for lag in range(half):
            late_share[chunk, :, lag * rows : (lag + 1) * rows] = lags[lag]
        late_share[chunk, :, lent : lent + width] = tap_share
        late_share[chunk, :, lent + width : lent + 2 * width] = conv_grad[0:8, :]
        send(
            late_share.at[chunk],
            late_landed.at[chunk],
            send_late,
            recv_landed.at[chunk],
            {"ctx": owner},
        )
        place = feature_out.at[:, columns(owner, chunk)]
        other = half - 1 - owner
        send(late_outbox.at[chunk, other], place, send_out, recv_out, {"ctx": half + other})
        pltpu.make_async_copy(late_outbox.at[chunk, owner], place, recv_out).start()

    def do_whole(chunk):
        landed = inbox.at[chunk]
        pltpu.make_async_copy(landed, landed, recv_in.at[chunk]).wait()
        tap_rows = tap_rows_of(me, chunk)
        wide_feat[0:8, :] = edge_zero
        lags = convolve(
            tap_rows,
            lambda block: inbox[chunk, blocks + block],
            lambda block: inbox[chunk, block],
            filters[pl.ds(pl.multiple_of(chunk * per_chunk, 8), per_chunk), :],
            blocks,
            blocks,
        )
        conv_grad[seq_len : seq_len + 8, :] = edge_zero
        tap_share = finish(tap_rows, blocks, put_out(chunk))
        keep_shares(chunk, lags, tap_share)
        for step in range(1, blocks):
            target = lax.rem(me + step, blocks)
            send(
                outbox.at[chunk, target], own_columns(chunk), send_out, recv_out, {"ctx": target}
            )
        pltpu.make_async_copy(outbox.at[chunk, me], own_columns(chunk), recv_out).start()
        send_shares(chunk)

    def drain(ref, sem):
        pltpu.make_async_copy(ref, ref, sem).wait()

    def do_chunk(chunk, carry):
        is_halved = chunk < halved

        @pl.when(jnp.logical_and(is_late, is_halved))
        def _():
            do_late(chunk)

        @pl.when(jnp.logical_and(is_early, is_halved))
        def _():
            do_early(chunk)

        @pl.when(jnp.logical_or(is_late, jnp.logical_not(is_halved)))
        def _():
            do_whole(chunk)

        return carry

    lax.fori_loop(0, chunks, do_chunk, 0)

    drain(shares.at[0 : dp_count - 1], recv_share)
    filter_scale = 1.0 / math.sqrt(dp_count * group * seq_len)
    tap_scale = 1.0 / math.sqrt(dp_count * seq_len)
    for chunk in range(chunks):
        total = shares[0, chunk]
        for rank in range(1, dp_count):
            total = total + shares[rank, chunk]
        filter_out[chunk * per_chunk : (chunk + 1) * per_chunk, :] = (
            total[:, :seq_len] * filter_scale
        )
        tap_out[:, chunk * width : (chunk + 1) * width] = total[:taps_count, seq_len:] * tap_scale
    drain(shares.at[0 : dp_count - 1], send_share)

    @pl.when(is_early)
    def _():
        drain(lent_filters, send_lent)
        drain(inbox.at[:, 0 : 2 * blocks - 1], send_in)
        drain(outbox.at[0:halved, 0 : half - 1], send_out)
        drain(outbox.at[halved:chunks, 0 : blocks - 1], send_out)

    @pl.when(me == half - 1)
    def _():
        for _ in range(half):
            drain(late_edge, send_edge)

    @pl.when(is_late)
    def _():
        drain(inbox.at[0:halved], send_in)
        drain(inbox.at[halved:chunks, 0 : 2 * blocks - 1], send_in)
        drain(outbox.at[:, 0 : blocks - 1], send_out)
        drain(outbox.at[0:halved, 0 : half - 1], send_out)
        drain(late_share, send_late)

    drain(outbox, recv_out)


def fused_body(arriving, features, short_taps, filters):
    blocks = lax.axis_size("ctx")
    dp_count = lax.axis_size("dp")
    pipe_count = lax.axis_size("pipe")
    rows, channels = features.shape[2], features.shape[3]
    own_width = channels // blocks
    filter_count, seq_len = filters.shape[1], filters.shape[2]
    group = own_width // filter_count
    taps_count = short_taps.shape[1]
    width = rows
    half = blocks // 2
    chunks = own_width // width
    per_chunk = width // group
    lent = half * rows
    halved = chunks // 2
    sizes = (blocks, dp_count, pipe_count, chunks, halved, rows, width, group, taps_count)
    anywhere = pl.BlockSpec(memory_space=pltpu.HBM)
    vmem = pl.BlockSpec(memory_space=pltpu.VMEM)
    one_sem = pltpu.SemaphoreType.DMA
    chunk_sems = pltpu.SemaphoreType.DMA((chunks,))
    feature_grads, filter_grads, tap_grads = pl.pallas_call(
        functools.partial(fused_kernel, sizes),
        out_shape=(
            jax.ShapeDtypeStruct((rows, channels), jnp.bfloat16),
            jax.ShapeDtypeStruct((filter_count, seq_len), jnp.float32),
            jax.ShapeDtypeStruct((taps_count, own_width), jnp.float32),
        ),
        in_specs=[anywhere] * 4,
        out_specs=(anywhere, vmem, vmem),
        scratch_shapes=[
            pltpu.VMEM((taps_count, channels // width, width), jnp.float32),
            pltpu.VMEM((filter_count, seq_len), jnp.float32),
            pltpu.VMEM((halved, per_chunk, lent), jnp.float32),
            pltpu.VMEM((chunks, 2 * blocks, rows, width), jnp.bfloat16),
            pltpu.VMEM((halved, 2 * half, rows, width), jnp.bfloat16),
            pltpu.VMEM((halved, 16, width), jnp.bfloat16),
            pltpu.VMEM((chunks, blocks, rows, width), jnp.bfloat16),
            pltpu.VMEM((halved, half, rows, width), jnp.bfloat16),
            pltpu.VMEM((dp_count, chunks, per_chunk, seq_len + width), jnp.float32),
            pltpu.VMEM((halved, per_chunk, lent + 2 * width), jnp.float32),
            pltpu.VMEM((halved, per_chunk, lent + 2 * width), jnp.float32),
            pltpu.VMEM((seq_len + 8, width), jnp.float32),
            pltpu.VMEM((2, width, seq_len), jnp.bfloat16),
            pltpu.VMEM((width, 2 * seq_len), jnp.bfloat16),
            pltpu.VMEM((per_chunk, seq_len), jnp.float32),
            pltpu.VMEM((width, seq_len), jnp.float32),
            pltpu.VMEM((seq_len + 8, width), jnp.float32),
            pltpu.VMEM((blocks * per_chunk * 8, width), jnp.float32),
            pltpu.SemaphoreType.DMA((2,)),
            one_sem,
            chunk_sems,
            chunk_sems,
            one_sem,
            chunk_sems,
            one_sem,
            chunk_sems,
            one_sem,
            chunk_sems,
            one_sem,
            one_sem,
            one_sem,
            one_sem,
        ],
        compiler_params=pltpu.CompilerParams(
            collective_id=0, has_side_effects=True, vmem_limit_bytes=60 * 1024 * 1024
        ),
    )(
        arriving[0, 0],
        features[0, 0],
        short_taps.reshape(taps_count, channels // width, width),
        filters,
    )
    return (feature_grads[None, None], filter_grads[None], tap_grads[None])


def fits_fused(mesh, features, short_taps, filters):
    blocks, rows = mesh.shape["ctx"], features.shape[2] // mesh.shape["ctx"]
    own_width = features.shape[3] // blocks
    own_filters = filters.shape[1] // blocks
    group = own_width // own_filters
    return (
        rows == 128
        and blocks == 4
        and mesh.shape["pipe"] == 2
        and own_width % (2 * rows) == 0
        and rows % group == 0
        and rows // group == 8
        and short_taps.shape[1] <= 8
    )


def solution(mesh):
    in_specs = (
        P("pipe", "dp", "ctx", None),
        P("pipe", "dp", "ctx", None),
        P("pipe", None, None),
        P("pipe", "ctx", None),
    )
    out_specs = (P("pipe", "dp", "ctx", None), P("pipe", "ctx", None), P("pipe", None, "ctx"))

    def run(arriving, features, short_taps, filters):
        chosen = fused_body if fits_fused(mesh, features, short_taps, filters) else body
        return jax.shard_map(
            chosen, mesh=mesh, in_specs=in_specs, out_specs=out_specs, check_vma=False
        )(arriving, features, short_taps, filters)

    return run
```

```python
import functools
import math

import jax
import jax.numpy as jnp
from jax import lax
from jax.experimental import pallas as pl
from jax.experimental.pallas import tpu as pltpu
from jax.sharding import PartitionSpec as P

TABLE_PRECISION = lax.Precision.HIGH
MESH = pl.DeviceIdType.MESH


def passed_along(value, axis, steps):
    count = lax.axis_size(axis)
    pairs = [(source, (source + steps) % count) for source in range(count)]
    return lax.ppermute(value, axis, pairs)


def phase_table(count_a, count_b, modulus):
    first_index = lax.broadcasted_iota(jnp.int32, (count_a, count_b), 0)
    second_index = lax.broadcasted_iota(jnp.int32, (count_a, count_b), 1)
    phase = (first_index * second_index % modulus).astype(jnp.float32) * (2.0 * math.pi / modulus)
    return (jnp.cos(phase), jnp.sin(phase))


def block_table(cos_part, sin_part):
    return jnp.stack(
        [
            jnp.concatenate([cos_part, -sin_part], axis=-1),
            jnp.concatenate([sin_part, cos_part], axis=-1),
        ]
    )


def split_length(seq_len):
    factor = 1
    for candidate in range(1, seq_len + 1):
        if seq_len % candidate == 0 and candidate * candidate <= 2 * seq_len:
            factor = candidate
    return factor


def finish_forward(first, inner_len, outer_len):
    full_len = inner_len * outer_len
    cos_turn, sin_turn = phase_table(inner_len, outer_len, full_len)
    first_re = first[..., :outer_len]
    first_im = first[..., outer_len:]
    turned = jnp.stack(
        [first_re * cos_turn + first_im * sin_turn, first_im * cos_turn - first_re * sin_turn],
        axis=-3,
    )
    cos_last, sin_last = phase_table(inner_len, inner_len, inner_len)
    return jnp.einsum(
        "...cnk,cne->...ke", turned, block_table(cos_last, sin_last), precision=TABLE_PRECISION
    )


def forward_pairs(values):
    inner_len = values.shape[-1]
    half_rows = values.shape[-2]
    outer_len = 2 * half_rows
    cos_first, sin_first = phase_table(half_rows, outer_len, outer_len)
    first = jnp.einsum(
        "fagmn,ame->fgne", values, block_table(cos_first, sin_first), precision=TABLE_PRECISION
    )
    return finish_forward(first, inner_len, outer_len)


def forward_real(values):
    inner_len = values.shape[-1]
    half_rows = values.shape[-2]
    outer_len = 2 * half_rows
    cos_first, sin_first = phase_table(half_rows, outer_len, outer_len)
    first = jnp.einsum(
        "fmn,me->fne", values, block_table(cos_first, sin_first)[0], precision=TABLE_PRECISION
    )
    return finish_forward(first, inner_len, outer_len)


def inverse_spectrum(spectrum, real_only):
    outer_len = spectrum.shape[-2]
    inner_len = spectrum.shape[-1] // 2
    half_rows = outer_len // 2
    full_len = outer_len * inner_len
    cos_first, sin_first = phase_table(inner_len, inner_len, inner_len)
    table_first = jnp.concatenate(
        [
            jnp.concatenate([cos_first, sin_first], axis=1),
            jnp.concatenate([-sin_first, cos_first], axis=1),
        ],
        axis=0,
    )
    step = jnp.einsum("...ke,ew->...kw", spectrum, table_first, precision=TABLE_PRECISION)
    step_re = step[..., :inner_len]
    step_im = step[..., inner_len:]
    cos_turn, sin_turn = phase_table(outer_len, inner_len, full_len)
    turned = jnp.stack(
        [step_re * cos_turn - step_im * sin_turn, step_re * sin_turn + step_im * cos_turn], axis=-3
    )
    cos_last, sin_last = phase_table(half_rows, outer_len, outer_len)
    table_last = jnp.stack(
        [jnp.stack([cos_last, -sin_last], axis=1), jnp.stack([sin_last, cos_last], axis=1)]
    )
    norm_factor = 1.0 / full_len
    if real_only:
        return (
            jnp.einsum("mck,...ckn->m...n", table_last[0], turned, precision=TABLE_PRECISION)
            * norm_factor
        )
    return (
        jnp.einsum("dmck,...ckn->dm...n", table_last, turned, precision=TABLE_PRECISION)
        * norm_factor
    )


def body(arriving, features, short_taps, filters):
    ctx_count = lax.axis_size("ctx")
    ctx_rank = lax.axis_index("ctx")
    dp_count = lax.axis_size("dp")
    rows_dev = features.shape[2]
    channels = features.shape[3]
    own_width = channels // ctx_count
    filter_count = filters.shape[1]
    group_size = own_width // filter_count
    half_group = group_size // 2
    taps_count = short_taps.shape[1]
    seq_len = filters.shape[2]
    inner_len = split_length(seq_len)
    half_rows = seq_len // inner_len
    feature_cols = features[0, 0].T
    arrived = passed_along(arriving, "pipe", -1)
    gradient_cols = arrived[0, 0].T
    gradient_block, feature_block = (
        lax.all_to_all(gradient_cols, "ctx", split_axis=0, concat_axis=1, tiled=True),
        lax.all_to_all(feature_cols, "ctx", split_axis=0, concat_axis=1, tiled=True),
    )
    tap_block = lax.dynamic_slice_in_dim(short_taps[0], ctx_rank * own_width, own_width, 1)
    feature_vals = feature_block.astype(jnp.float32)
    padded_feat = jnp.pad(feature_vals, ((0, 0), (taps_count - 1, 0)))
    conv_in = jnp.zeros(feature_vals.shape, jnp.float32)
    for offset in range(taps_count):
        conv_in = (
            conv_in
            + tap_block[offset][:, None]
            * padded_feat[:, taps_count - 1 - offset : taps_count - 1 - offset + seq_len]
        )
    pair_shape = (filter_count, 2, half_group, half_rows, inner_len)
    spectrum_u = forward_pairs(conv_in.reshape(pair_shape))
    spectrum_g = forward_pairs(gradient_block.astype(jnp.float32).reshape(pair_shape))
    spectrum_h = forward_real(filters[0].reshape(filter_count, half_rows, inner_len))[:, None]
    g_re = spectrum_g[..., :inner_len]
    g_im = spectrum_g[..., inner_len:]
    u_re = spectrum_u[..., :inner_len]
    u_im = spectrum_u[..., inner_len:]
    h_re = spectrum_h[..., :inner_len]
    h_im = spectrum_h[..., inner_len:]
    back = jnp.concatenate([h_re * g_re + h_im * g_im, h_re * g_im - h_im * g_re], axis=-1)
    lag = jnp.concatenate(
        [jnp.sum(g_re * u_re + g_im * u_im, axis=1), jnp.sum(g_im * u_re - g_re * u_im, axis=1)],
        axis=-1,
    )
    grad_blocks = inverse_spectrum(back, False)
    conv_in_grad = jnp.transpose(grad_blocks, (2, 0, 3, 1, 4)).reshape(own_width, seq_len)
    filter_part = jnp.transpose(inverse_spectrum(lag, True), (1, 0, 2)).reshape(
        filter_count, seq_len
    )
    padded_grad = jnp.pad(conv_in_grad, ((0, 0), (0, taps_count - 1)))
    feature_grad = jnp.zeros(conv_in_grad.shape, jnp.float32)
    tap_terms = []
    for offset in range(taps_count):
        feature_grad = (
            feature_grad + tap_block[offset][:, None] * padded_grad[:, offset : offset + seq_len]
        )
        tap_terms.append(
            jnp.sum(
                conv_in_grad
                * padded_feat[:, taps_count - 1 - offset : taps_count - 1 - offset + seq_len],
                axis=1,
            )
        )
    tap_part = jnp.stack(tap_terms)
    filter_total, tap_total = lax.psum((filter_part, tap_part), "dp")
    back_cols = feature_grad.astype(jnp.bfloat16)
    feature_rows = lax.all_to_all(back_cols, "ctx", split_axis=1, concat_axis=0, tiled=True)
    feature_grads = feature_rows.T.reshape(1, 1, rows_dev, channels)
    filter_scale = 1.0 / math.sqrt(dp_count * group_size * seq_len)
    tap_scale = 1.0 / math.sqrt(dp_count * seq_len)
    filter_grads = (filter_total * filter_scale)[None]
    tap_grads = (tap_total * tap_scale).reshape(1, taps_count, own_width)
    return (feature_grads, filter_grads, tap_grads)


def fused_kernel(
    sizes,
    arriving,
    features,
    taps_all,
    filters_all,
    feature_out,
    filter_out,
    tap_out,
    taps,
    filters,
    lent_filters,
    inbox,
    late_inbox,
    late_edge,
    outbox,
    late_outbox,
    shares,
    late_share,
    late_landed,
    wide_feat,
    split_in,
    grad_cols,
    turned,
    conv_cols,
    conv_grad,
    diagonals,
    local_sems,
    send_in,
    recv_in,
    recv_late,
    send_edge,
    recv_edge,
    send_lent,
    recv_lent,
    send_late,
    recv_landed,
    send_out,
    recv_out,
    send_share,
    recv_share,
):
    blocks, dp_count, pipe_count, chunks, halved, rows, width, group, taps_count = sizes
    seq_len = blocks * rows
    half = blocks // 2
    own_width = chunks * width
    per_chunk = width // group
    me = lax.axis_index("ctx")
    dp_rank = lax.axis_index("dp")
    pipe_rank = lax.axis_index("pipe")
    before = lax.rem(pipe_rank + pipe_count - 1, pipe_count)
    is_early = me < half
    is_late = me >= half

    fetch_taps = pltpu.make_async_copy(taps_all, taps, local_sems.at[0])
    fetch_taps.start()
    fetch_filters = pltpu.make_async_copy(filters_all.at[0], filters, local_sems.at[1])
    fetch_filters.start()

    barrier = pltpu.get_barrier_semaphore()
    for step in range(1, blocks):
        pl.semaphore_signal(
            barrier,
            inc=1,
            device_id={"ctx": lax.rem(me + step, blocks)},
            device_id_type=MESH,
        )
    for step in range(blocks):
        pl.semaphore_signal(
            barrier,
            inc=1,
            device_id={"pipe": before, "ctx": lax.rem(me + step, blocks)},
            device_id_type=MESH,
        )
    for step in range(1, dp_count):
        pl.semaphore_signal(
            barrier,
            inc=1,
            device_id={"dp": lax.rem(dp_rank + step, dp_count)},
            device_id_type=MESH,
        )
    pl.semaphore_wait(barrier, 2 * blocks + dp_count - 2)

    def columns(owner, chunk):
        return pl.ds(pl.multiple_of(owner * own_width + chunk * width, width), width)

    def tap_rows_of(owner, chunk):
        place = owner * chunks + chunk
        return [taps[tap, pl.ds(place, 1), :] for tap in range(taps_count)]

    def send(source, target, send_sem, recv_sem, device):
        pltpu.make_async_remote_copy(
            src_ref=source,
            dst_ref=target,
            send_sem=send_sem,
            recv_sem=recv_sem,
            device_id=device,
            device_id_type=MESH,
        ).start()

    def send_chunk(chunk, carry):
        is_halved = chunk < halved

        @pl.when(jnp.logical_and(is_early, is_halved))
        def _():
            send(
                filters_all.at[0, pl.ds(pl.multiple_of(chunk * per_chunk, 8), per_chunk), 0 : half * rows],
                lent_filters.at[chunk],
                send_lent,
                recv_lent.at[chunk],
                {"ctx": me + half},
            )

        @pl.when(jnp.logical_and(me == half - 1, is_halved))
        def _():
            for owner in range(half):
                send(
                    features.at[rows - 16 : rows, columns(owner, chunk)],
                    late_edge.at[chunk],
                    send_edge,
                    recv_edge.at[chunk],
                    {"ctx": half + owner},
                )

        @pl.when(jnp.logical_and(is_late, is_halved))
        def _():
            for step in range(half):
                owner = lax.rem(me + step, half)
                device = owner + half
                send(
                    arriving.at[:, columns(owner, chunk)],
                    late_inbox.at[chunk, me - half],
                    send_in,
                    recv_late.at[chunk],
                    {"pipe": before, "ctx": device},
                )
                if step:
                    send(
                        features.at[:, columns(owner, chunk)],
                        late_inbox.at[chunk, me],
                        send_in,
                        recv_late.at[chunk],
                        {"ctx": device},
                    )
                else:
                    pltpu.make_async_copy(
                        features.at[:, columns(owner, chunk)],
                        late_inbox.at[chunk, me],
                        recv_late.at[chunk],
                    ).start()

        for step in range(blocks):
            target = lax.rem(me + step, blocks)
            send(
                arriving.at[:, columns(target, chunk)],
                inbox.at[chunk, me],
                send_in,
                recv_in.at[chunk],
                {"pipe": before, "ctx": target},
            )
            if step:

                @pl.when(
                    jnp.logical_or(
                        jnp.logical_or(is_early, target >= half), jnp.logical_not(is_halved)
                    )
                )
                def _():
                    send(
                        features.at[:, columns(target, chunk)],
                        inbox.at[chunk, blocks + me],
                        send_in,
                        recv_in.at[chunk],
                        {"ctx": target},
                    )

        pltpu.make_async_copy(
            features.at[:, columns(me, chunk)], inbox.at[chunk, blocks + me], recv_in.at[chunk]
        ).start()
        return carry

    lax.fori_loop(0, chunks, send_chunk, 0)
    fetch_taps.wait()
    fetch_filters.wait()

    row_index = lax.broadcasted_iota(jnp.int32, (rows, rows), 0)
    lane_index = lax.broadcasted_iota(jnp.int32, (rows, rows), 1)
    upper = lane_index >= row_index
    lower = row_index >= lane_index
    mirror = (lax.rem(row_index + lane_index, rows) == 0).astype(jnp.bfloat16)
    zero_tile = jnp.zeros((rows, rows), jnp.float32)
    edge_zero = jnp.zeros((8, width), jnp.float32)

    def convolve(tap_rows, feat_at, grad_at, kernel_rows, feat_blocks, grad_blocks):
        for block in range(feat_blocks):
            wide_feat[8 + block * rows : 8 + (block + 1) * rows, :] = feat_at(block).astype(
                jnp.float32
            )
        for block in range(feat_blocks):
            here = slice(block * rows, (block + 1) * rows)
            summed = zero_tile
            for tap in range(taps_count):
                start = 8 + block * rows - tap
                summed = summed + tap_rows[tap] * wide_feat[start : start + rows, :]
            summed = summed.T
            high = summed.astype(jnp.bfloat16)
            split_in[0, :, here] = high
            split_in[1, :, here] = (summed - high.astype(jnp.float32)).astype(jnp.bfloat16)
        for block in range(grad_blocks):
            grad_cols[:, block * rows : (block + 1) * rows] = grad_at(block).T
        grad_cols[:, grad_blocks * rows : (grad_blocks + feat_blocks - 1) * rows] = jnp.zeros(
            (width, (feat_blocks - 1) * rows), jnp.bfloat16
        )
        for block in range(grad_blocks):
            here = slice(block * rows, (block + 1) * rows)
            whole = kernel_rows[:, here]
            high = whole.astype(jnp.bfloat16)
            low = (whole - high.astype(jnp.float32)).astype(jnp.bfloat16)
            turned[:, here] = jnp.dot(
                high, mirror, preferred_element_type=jnp.float32
            ) + jnp.dot(low, mirror, preferred_element_type=jnp.float32)

        def one_filter(index):
            ours = pl.ds(pl.multiple_of(index * group, group), group)
            kernel_row = turned[pl.ds(index, 1), :]
            highs, lows = [], []
            last = zero_tile
            for block in range(grad_blocks):
                spread = jnp.broadcast_to(
                    kernel_row[:, block * rows : (block + 1) * rows], (rows, rows)
                )
                rolled = pltpu.roll(spread, 0, 1, stride=1, stride_axis=0)
                tile = jnp.where(lower, rolled, last)
                last = rolled
                high = tile.astype(jnp.bfloat16)
                highs.append(high)
                lows.append((tile - high.astype(jnp.float32)).astype(jnp.bfloat16))
            table = jnp.concatenate(
                [jnp.concatenate(highs, axis=0), jnp.concatenate(lows, axis=0)], axis=1
            )
            shifted = jnp.concatenate(
                [
                    grad_cols[ours, block * rows : (block + grad_blocks) * rows]
                    for block in range(feat_blocks)
                ],
                axis=0,
            )
            product = jnp.dot(shifted, table, preferred_element_type=jnp.float32)
            both = product[:, :rows] + product[:, rows:]
            for block in range(feat_blocks):
                conv_cols[ours, block * rows : (block + 1) * rows] = both[
                    block * group : (block + 1) * group
                ]
            picked = jnp.concatenate(
                [
                    split_in[part, ours, block * rows : (block + 1) * rows]
                    for part in range(2)
                    for block in range(feat_blocks)
                ],
                axis=0,
            )
            sums = jnp.dot(
                picked.T,
                jnp.concatenate([shifted, shifted], axis=0),
                preferred_element_type=jnp.float32,
            )
            for lag in range(grad_blocks):
                following = (
                    sums[:, (lag + 1) * rows : (lag + 2) * rows]
                    if lag + 1 < grad_blocks
                    else zero_tile
                )
                merged = jnp.where(upper, sums[:, lag * rows : (lag + 1) * rows], following)
                folded = [merged[0:8]]
                for part in range(1, rows // 8):
                    folded.append(
                        pltpu.roll(merged[part * 8 : part * 8 + 8], rows - part * 8, 1)
                    )
                while len(folded) > 1:
                    folded = [
                        folded[place] + folded[place + 1] for place in range(0, len(folded), 2)
                    ]
                place = pl.multiple_of((lag * per_chunk + index) * 8, 8)
                diagonals[pl.ds(place, 8), :] = folded[0]

        def do_filters(index, inner):
            for place in range(4):
                one_filter(4 * index + place)
            return inner

        lax.fori_loop(0, per_chunk // 4, do_filters, 0)
        for block in range(feat_blocks):
            here = slice(block * rows, (block + 1) * rows)
            conv_grad[here, :] = conv_cols[:, here].T
        count = grad_blocks * per_chunk
        lagged = diagonals[pl.ds(0, count, stride=8), :]
        for turn in range(1, 8):
            lagged = lagged + pltpu.roll(
                diagonals[pl.ds(turn, count, stride=8), :], rows - turn, 1
            )
        return [
            lagged[lag * per_chunk : (lag + 1) * per_chunk] for lag in range(grad_blocks)
        ]

    def finish(tap_rows, feat_blocks, put):
        tap_sums = [edge_zero] * taps_count
        for block in range(feat_blocks):
            here = block * rows
            summed = zero_tile
            feats = wide_feat[8 + here : 8 + here + rows, :]
            for tap in range(taps_count):
                grads = conv_grad[here + tap : here + tap + rows, :]
                summed = summed + tap_rows[tap] * grads
                pairs = grads * feats
                tap_sums[tap] = tap_sums[tap] + jnp.sum(
                    pairs.reshape(rows // 8, 8, width), axis=0
                )
            put(block, summed.astype(jnp.bfloat16))
        tap_sums = [jnp.sum(value, axis=0, keepdims=True) for value in tap_sums]
        if per_chunk > taps_count:
            tap_sums.append(jnp.zeros((per_chunk - taps_count, width), jnp.float32))
        return jnp.concatenate(tap_sums, axis=0)


    def put_out(chunk):
        def put(block, value):
            outbox[chunk, block] = value

        return put

    def keep_shares(chunk, lags, tap_share):
        for lag in range(blocks):
            shares[dp_rank, chunk, :, lag * rows : (lag + 1) * rows] = lags[lag]
        shares[dp_rank, chunk, :, seq_len : seq_len + width] = tap_share

    def send_shares(chunk):
        for step in range(1, dp_count):
            send(
                shares.at[dp_rank, chunk],
                shares.at[dp_rank, chunk],
                send_share,
                recv_share,
                {"dp": lax.rem(dp_rank + step, dp_count)},
            )

    def own_columns(chunk):
        return feature_out.at[:, columns(me, chunk)]

    def do_early(chunk):
        landed = inbox.at[chunk, 0 : blocks + half]
        pltpu.make_async_copy(landed, landed, recv_in.at[chunk]).wait()
        tap_rows = tap_rows_of(me, chunk)
        wide_feat[0:8, :] = edge_zero
        lags = convolve(
            tap_rows,
            lambda block: inbox[chunk, blocks + block],
            lambda block: inbox[chunk, block],
            filters[pl.ds(pl.multiple_of(chunk * per_chunk, 8), per_chunk), :],
            half,
            blocks,
        )
        bundle = late_landed.at[chunk]
        pltpu.make_async_copy(bundle, bundle, recv_landed.at[chunk]).wait()
        lent = half * rows
        conv_grad[lent : lent + 8, :] = late_landed[chunk, :, lent + width : lent + 2 * width]
        tap_share = finish(tap_rows, half, put_out(chunk))
        tap_share = tap_share + late_landed[chunk, :, lent : lent + width]
        for lag in range(half):
            lags[lag] = lags[lag] + late_landed[chunk, :, lag * rows : (lag + 1) * rows]
        keep_shares(chunk, lags, tap_share)
        other = half - 1 - me
        send(outbox.at[chunk, other], own_columns(chunk), send_out, recv_out, {"ctx": other})
        pltpu.make_async_copy(outbox.at[chunk, me], own_columns(chunk), recv_out).start()
        send_shares(chunk)

    def do_late(chunk):
        owner = me - half
        landed = late_inbox.at[chunk]
        pltpu.make_async_copy(landed, landed, recv_late.at[chunk]).wait()
        edge = late_edge.at[chunk]
        pltpu.make_async_copy(edge, edge, recv_edge.at[chunk]).wait()
        lent_here = lent_filters.at[chunk]
        pltpu.make_async_copy(lent_here, lent_here, recv_lent.at[chunk]).wait()
        tap_rows = tap_rows_of(owner, chunk)
        wide_feat[0:8, :] = late_edge[chunk].astype(jnp.float32)[8:16]
        lags = convolve(
            tap_rows,
            lambda block: late_inbox[chunk, half + block],
            lambda block: late_inbox[chunk, block],
            lent_filters[chunk],
            half,
            half,
        )
        conv_grad[half * rows : half * rows + 8, :] = edge_zero

        def put(block, value):
            late_outbox[chunk, block] = value

        tap_share = finish(tap_rows, half, put)
        lent = half * rows
        for lag in range(half):
            late_share[chunk, :, lag * rows : (lag + 1) * rows] = lags[lag]
        late_share[chunk, :, lent : lent + width] = tap_share
        late_share[chunk, :, lent + width : lent + 2 * width] = conv_grad[0:8, :]
        send(
            late_share.at[chunk],
            late_landed.at[chunk],
            send_late,
            recv_landed.at[chunk],
            {"ctx": owner},
        )
        place = feature_out.at[:, columns(owner, chunk)]
        other = half - 1 - owner
        send(late_outbox.at[chunk, other], place, send_out, recv_out, {"ctx": half + other})
        pltpu.make_async_copy(late_outbox.at[chunk, owner], place, recv_out).start()

    def do_whole(chunk):
        landed = inbox.at[chunk]
        pltpu.make_async_copy(landed, landed, recv_in.at[chunk]).wait()
        tap_rows = tap_rows_of(me, chunk)
        wide_feat[0:8, :] = edge_zero
        lags = convolve(
            tap_rows,
            lambda block: inbox[chunk, blocks + block],
            lambda block: inbox[chunk, block],
            filters[pl.ds(pl.multiple_of(chunk * per_chunk, 8), per_chunk), :],
            blocks,
            blocks,
        )
        conv_grad[seq_len : seq_len + 8, :] = edge_zero
        tap_share = finish(tap_rows, blocks, put_out(chunk))
        keep_shares(chunk, lags, tap_share)
        for step in range(1, blocks):
            target = lax.rem(me + step, blocks)
            send(
                outbox.at[chunk, target], own_columns(chunk), send_out, recv_out, {"ctx": target}
            )
        pltpu.make_async_copy(outbox.at[chunk, me], own_columns(chunk), recv_out).start()
        send_shares(chunk)

    def drain(ref, sem):
        pltpu.make_async_copy(ref, ref, sem).wait()

    def do_chunk(chunk, carry):
        is_halved = chunk < halved

        @pl.when(jnp.logical_and(is_late, is_halved))
        def _():
            do_late(chunk)

        @pl.when(jnp.logical_and(is_early, is_halved))
        def _():
            do_early(chunk)

        @pl.when(jnp.logical_or(is_late, jnp.logical_not(is_halved)))
        def _():
            do_whole(chunk)

        return carry

    lax.fori_loop(0, chunks, do_chunk, 0)

    drain(shares.at[0 : dp_count - 1], recv_share)
    filter_scale = 1.0 / math.sqrt(dp_count * group * seq_len)
    tap_scale = 1.0 / math.sqrt(dp_count * seq_len)
    for chunk in range(chunks):
        total = shares[0, chunk]
        for rank in range(1, dp_count):
            total = total + shares[rank, chunk]
        filter_out[chunk * per_chunk : (chunk + 1) * per_chunk, :] = (
            total[:, :seq_len] * filter_scale
        )
        tap_out[:, chunk, :] = total[:taps_count, seq_len:] * tap_scale
    drain(shares.at[0 : dp_count - 1], send_share)

    @pl.when(is_early)
    def _():
        drain(lent_filters, send_lent)
        drain(inbox.at[:, 0 : 2 * blocks - 1], send_in)
        drain(outbox.at[0:halved, 0 : half - 1], send_out)
        drain(outbox.at[halved:chunks, 0 : blocks - 1], send_out)

    @pl.when(me == half - 1)
    def _():
        for _ in range(half):
            drain(late_edge, send_edge)

    @pl.when(is_late)
    def _():
        drain(inbox.at[0:halved], send_in)
        drain(inbox.at[halved:chunks, 0 : 2 * blocks - 1], send_in)
        drain(outbox.at[:, 0 : blocks - 1], send_out)
        drain(outbox.at[0:halved, 0 : half - 1], send_out)
        drain(late_share, send_late)

    drain(outbox, recv_out)


def fused_body(arriving, features, short_taps, filters):
    blocks = lax.axis_size("ctx")
    dp_count = lax.axis_size("dp")
    pipe_count = lax.axis_size("pipe")
    rows, channels = features.shape[2], features.shape[3]
    own_width = channels // blocks
    filter_count, seq_len = filters.shape[1], filters.shape[2]
    group = own_width // filter_count
    taps_count = short_taps.shape[1]
    width = rows
    half = blocks // 2
    chunks = own_width // width
    per_chunk = width // group
    lent = half * rows
    halved = chunks // 2
    sizes = (blocks, dp_count, pipe_count, chunks, halved, rows, width, group, taps_count)
    anywhere = pl.BlockSpec(memory_space=pltpu.HBM)
    vmem = pl.BlockSpec(memory_space=pltpu.VMEM)
    one_sem = pltpu.SemaphoreType.DMA
    chunk_sems = pltpu.SemaphoreType.DMA((chunks,))
    feature_grads, filter_grads, tap_grads = pl.pallas_call(
        functools.partial(fused_kernel, sizes),
        out_shape=(
            jax.ShapeDtypeStruct((rows, channels), jnp.bfloat16),
            jax.ShapeDtypeStruct((filter_count, seq_len), jnp.float32),
            jax.ShapeDtypeStruct((taps_count, chunks, width), jnp.float32),
        ),
        in_specs=[anywhere] * 4,
        out_specs=(anywhere, vmem, vmem),
        scratch_shapes=[
            pltpu.VMEM((taps_count, channels // width, width), jnp.float32),
            pltpu.VMEM((filter_count, seq_len), jnp.float32),
            pltpu.VMEM((halved, per_chunk, lent), jnp.float32),
            pltpu.VMEM((chunks, 2 * blocks, rows, width), jnp.bfloat16),
            pltpu.VMEM((halved, 2 * half, rows, width), jnp.bfloat16),
            pltpu.VMEM((halved, 16, width), jnp.bfloat16),
            pltpu.VMEM((chunks, blocks, rows, width), jnp.bfloat16),
            pltpu.VMEM((halved, half, rows, width), jnp.bfloat16),
            pltpu.VMEM((dp_count, chunks, per_chunk, seq_len + width), jnp.float32),
            pltpu.VMEM((halved, per_chunk, lent + 2 * width), jnp.float32),
            pltpu.VMEM((halved, per_chunk, lent + 2 * width), jnp.float32),
            pltpu.VMEM((seq_len + 8, width), jnp.float32),
            pltpu.VMEM((2, width, seq_len), jnp.bfloat16),
            pltpu.VMEM((width, 2 * seq_len), jnp.bfloat16),
            pltpu.VMEM((per_chunk, seq_len), jnp.float32),
            pltpu.VMEM((width, seq_len), jnp.float32),
            pltpu.VMEM((seq_len + 8, width), jnp.float32),
            pltpu.VMEM((blocks * per_chunk * 8, width), jnp.float32),
            pltpu.SemaphoreType.DMA((2,)),
            one_sem,
            chunk_sems,
            chunk_sems,
            one_sem,
            chunk_sems,
            one_sem,
            chunk_sems,
            one_sem,
            chunk_sems,
            one_sem,
            one_sem,
            one_sem,
            one_sem,
        ],
        compiler_params=pltpu.CompilerParams(
            collective_id=0, has_side_effects=True, vmem_limit_bytes=60 * 1024 * 1024
        ),
    )(
        arriving[0, 0],
        features[0, 0],
        short_taps.reshape(taps_count, channels // width, width),
        filters,
    )
    return (
        feature_grads[None, None],
        filter_grads[None],
        tap_grads.reshape(1, taps_count, own_width),
    )


def fits_fused(mesh, features, short_taps, filters):
    blocks, rows = mesh.shape["ctx"], features.shape[2] // mesh.shape["ctx"]
    own_width = features.shape[3] // blocks
    own_filters = filters.shape[1] // blocks
    group = own_width // own_filters
    return (
        rows == 128
        and blocks == 4
        and mesh.shape["pipe"] == 2
        and own_width % (2 * rows) == 0
        and rows % group == 0
        and rows // group == 8
        and short_taps.shape[1] <= 8
    )


def solution(mesh):
    in_specs = (
        P("pipe", "dp", "ctx", None),
        P("pipe", "dp", "ctx", None),
        P("pipe", None, None),
        P("pipe", "ctx", None),
    )
    out_specs = (P("pipe", "dp", "ctx", None), P("pipe", "ctx", None), P("pipe", None, "ctx"))

    def run(arriving, features, short_taps, filters):
        chosen = fused_body if fits_fused(mesh, features, short_taps, filters) else body
        return jax.shard_map(
            chosen, mesh=mesh, in_specs=in_specs, out_specs=out_specs, check_vma=False
        )(arriving, features, short_taps, filters)

    return run
```
